32 devices in a mesh: tiles: 8 (over y, x, core), nodes: 4 (over z).
Axes of the slice: x: 2, y: 2, z: 4, core: 2. Of those that a mesh axis runs over, the one named last changes fastest.
Arguments:
- images: bfloat16 [512, 128, 128], P(('tiles', 'nodes')), may hold values from -6 to 6
- direction: float32 [4096, 3, 128], P(('tiles', 'nodes')), may hold values from -6 to 6
- damping: float32 [4096, 3, 128], P(('tiles', 'nodes')), may hold values from 0.5 to 4
- calibration: float32 [4, 2, 3], replicated, may hold values from -3 to 3
- camera: int32 [512], P(('tiles', 'nodes')), may hold values from 0 to 3
- owners: int32 [512, 16], P(('tiles', 'nodes')), may hold values from 0 to 31, all different within a row; in each aligned block of 16 rows (0 to 15, 16 to 31, ...) at most 16 rows name the same one
- local_block: int32 [512, 16], P(('tiles', 'nodes')), may hold values from 0 to 127
- connect: int32 [512, 4, 1024], P(('tiles', 'nodes')), may hold values from 0 to 2047
Outputs:
- product: float32 [4096, 3, 128], P(('tiles', 'nodes'))
The draws below stay inside these ranges and needn't reach their ends.
Inputs may be any that keep to these rules, and one draw needn't show every extreme that they name: Within the rows of one device (aligned blocks of 16 tiles) each owner is named by at most 16 tiles, and exactly 16 in some block; a tile names 16 different owners.
All inputs are finite; a program needn't handle non-finite values.
Results may differ from the reference program's by a relative error of at most 0.0003.
Values sent between devices are 32-bit elements; how exact they have to be, the bound alone decides.
No kernel may reach another device: no remote copies, remote signals or barrier semaphores. Data moves between devices by JAX's collectives and lax.ppermute only.
A program may use at most 256 MiB of HBM per device.

```python
import math
import jax
import jax.numpy as jnp
import numpy as np
from jax import lax

TILE_DEV = 16
BLK_DEV = 128
MAXB = 16
NBS = 128
TPX = 128
EPX = 4
NCAM = 4
ELEMS = 1024
TILES = 512
NBLOCKS = 4096
OWNERS = 32
CAP = 16


def set_ends(array, key, smallest, largest):
    place = [jax.random.randint(jax.random.fold_in(key, axis), (), 0, length) for axis, length in enumerate(array.shape)]
    main_axis = array.shape.index(max(array.shape))
    next_to = place[:main_axis] + [(place[main_axis] + 1) % array.shape[main_axis]] + place[main_axis + 1:]
    return array.at[tuple(place)].set(smallest).at[tuple(next_to)].set(largest)


def steps_of(rng, shape, pieces, low, top_value):
    gain = 1.0
    for axis_at, blocks in pieces:
        draws = jax.random.uniform(jax.random.fold_in(jax.random.fold_in(rng, 6), axis_at), (blocks,), jnp.float32, low / len(pieces), top_value / len(pieces))
        gain = gain * jnp.repeat(jnp.exp(draws), shape[axis_at] // blocks).reshape((-1,) + (1,) * (len(shape) - 1 - axis_at))
    return gain


def assign_block(key, own, number, rows, amount, top, bound, lean):
    ranking = jax.random.permutation(key, amount)
    crowded, ordinary = portions_of(amount, rows * top, bound, lean, True), portions_of(amount, rows * top, bound, lean, False)
    places = jnp.arange(amount)

    def named(lengths, turn):
        used = int((lengths > 0).sum())
        fixed = max(1, used // 4)
        moved = fixed + (places - fixed + turn * (used - fixed)) % max(1, amount - fixed)
        return jnp.zeros((amount,), jnp.int32).at[ranking[jnp.where(places < fixed, places, moved)]].set(jnp.asarray(lengths, jnp.int32))

    lengths = jnp.where(number % 4 == 0, named(crowded, number // 4), named(ordinary, number - number // 4 - 1))
    mixed = jax.random.permutation(jax.random.fold_in(own, 3), amount)
    source_of, taker = mixed[0:amount // 2 * 2:2], mixed[1:amount // 2 * 2:2]
    margin = jnp.minimum(lengths[source_of] - 1, bound - lengths[taker]) // 2
    margin = jnp.where((source_of == ranking[0]) | (taker == ranking[0]) | (lengths[taker] == 0), 0, jnp.maximum(margin, 0))
    moved = jax.random.randint(jax.random.fold_in(own, 4), (amount // 2,), 0, 1 << 20) % (margin + 1)
    lengths = lengths.at[source_of].add(-moved).at[taker].add(moved)
    members = jnp.searchsorted(jnp.cumsum(lengths), jnp.arange(rows * top), side="right").astype(jnp.int32)
    listing = members.reshape(top, rows).T
    listing = listing[jax.random.permutation(jax.random.fold_in(own, 1), rows)]
    turn = jax.random.randint(jax.random.fold_in(own, 2), (rows, 1), 0, top)
    return jnp.take_along_axis(listing, (jnp.arange(top)[None, :] + turn) % top, axis=1)


def portions_of(count, total, limit, slope, full):
    weights = [(1 << 20) // math.isqrt(rank ** slope) + 1 for rank in range(1, count + 1)]
    largest = limit if full else min(limit, max(-(-total // count), total * weights[0] // sum(weights)))
    least = 1 if total - largest >= count - 1 else 0
    holding, spare = [largest] + [least] * (count - 1), total - largest - least * (count - 1)
    while spare > 0:
        free = [i for i in range(1, count) if holding[i] < largest] or [i for i in range(1, count) if holding[i] < limit]
        whole, remaining = sum([weights[i] for i in free]), spare
        for i in free:
            more = min(limit - holding[i], max(1, remaining * weights[i] // whole), spare)
            holding[i] = holding[i] + more
            spare = spare - more
    return np.array(holding)


def normal_values(own_key, shape, scale, most, pieces=(), kind=jnp.bfloat16):
    values = scale * jax.random.normal(own_key, shape, jnp.float32)
    if pieces:
        values = values * steps_of(own_key, shape, pieces, -0.22, 0.18)
    return jnp.clip(values, -most, most).astype(kind)


def setup_inputs(seed: int = 0) -> dict:
    seeds = jax.random.split(jax.random.key(seed), 9)
    images = normal_values(seeds[0], (TILES, TPX, TPX), 1.0, 6.0, ((0, 32),))
    direction = normal_values(seeds[1], (NBLOCKS, 3, NBS), 1.0, 6.0, ((0, 32),), jnp.float32)
    damping = jnp.clip(jnp.exp(math.log(4.0) - 2.0794415 * jax.random.uniform(seeds[2], (NBLOCKS, 3, NBS), jnp.float32) ** steps_of(seeds[2], (NBLOCKS, 3, NBS), ((0, 32),), -0.2, 0.2)), 0.5, 4.0)
    calibration = normal_values(seeds[3], (NCAM, 2, 3), 1.0, 3.0, (), jnp.float32)
    camera = set_ends(jax.random.randint(seeds[4], (TILES,), 0, NCAM), jax.random.fold_in(seeds[4], 1), 0, NCAM - 1).astype(jnp.int32)
    owners_keys = jax.random.split(jax.random.fold_in(seeds[5], 1), TILES // TILE_DEV)
    owners_turns = jax.random.permutation(jax.random.fold_in(seeds[5], 3), TILES // TILE_DEV)
    owners = jax.vmap(lambda own, number: assign_block(jax.random.fold_in(seeds[5], 2), own, number, TILE_DEV, OWNERS, MAXB, CAP, 2))(owners_keys, owners_turns).reshape((TILES, MAXB))
    local_block = set_ends(jax.random.randint(seeds[6], (TILES, MAXB), 0, BLK_DEV), jax.random.fold_in(seeds[6], 1), 0, BLK_DEV - 1).astype(jnp.int32)
    connect = set_ends(jax.random.randint(seeds[7], (TILES, 4, ELEMS), 0, MAXB * NBS), jax.random.fold_in(seeds[7], 1), 0, (MAXB * NBS) - 1).astype(jnp.int32)
    return {"images": images, "direction": direction, "damping": damping, "calibration": calibration, "camera": camera, "owners": owners, "local_block": local_block, "connect": connect}


group_tiles = 8


def shape_table():
    position = (jnp.arange(EPX, dtype=jnp.float32) + 0.5) / EPX
    across = position[None, :]
    downward = position[:, None]
    return jnp.stack([(1.0 - across) * (1.0 - downward), across * (1.0 - downward), (1.0 - across) * downward, across * downward])


def slopes(pixels):
    slope_x = jnp.concatenate([pixels[:, :, 1:2] - pixels[:, :, 0:1], 0.5 * (pixels[:, :, 2:] - pixels[:, :, :-2]), pixels[:, :, -1:] - pixels[:, :, -2:-1]], axis=2)
    slope_y = jnp.concatenate([pixels[:, 1:2, :] - pixels[:, 0:1, :], 0.5 * (pixels[:, 2:, :] - pixels[:, :-2, :]), pixels[:, -1:, :] - pixels[:, -2:-1, :]], axis=1)
    return slope_x, slope_y


def to_elements(plane):
    tile_count = plane.shape[0]
    side_cells = plane.shape[1] // EPX
    return plane.reshape(tile_count, side_cells, EPX, side_cells, EPX).transpose(0, 2, 4, 1, 3).reshape(tile_count, EPX, EPX, side_cells * side_cells)


def tile_terms(slope_x, slope_y, projection, nodal_values, link_ids, weights):
    corners = jax.vmap(lambda values, indices: values[:, indices])(nodal_values, link_ids)
    displaced = corners[:, :, 0, None, None, :] * weights[0][None, None, :, :, None]
    for corner in range(1, 4):
        displaced = displaced + corners[:, :, corner, None, None, :] * weights[corner][None, None, :, :, None]

    def image_motion(motion_axis):
        result = projection[:, motion_axis, 0, None, None, None] * displaced[:, 0]
        result = result + projection[:, motion_axis, 1, None, None, None] * displaced[:, 1]
        return result + projection[:, motion_axis, 2, None, None, None] * displaced[:, 2]

    change = slope_x * image_motion(0) + slope_y * image_motion(1)
    force_x = slope_x * change
    force_y = slope_y * change
    pushed = jnp.stack([projection[:, 0, component, None, None, None] * force_x + projection[:, 1, component, None, None, None] * force_y for component in range(3)], axis=1)
    gathered = jnp.sum(pushed[:, :, None] * weights[None, None, :, :, :, None], axis=(3, 4))
    node_slots = nodal_values.shape[2]

    def spread(contribution, indices):
        return jnp.zeros((3, node_slots), jnp.float32).at[:, indices.reshape(-1)].add(contribution.reshape(3, -1))

    return jax.vmap(spread)(gathered, link_ids)


def reference(images, direction, damping, calibration, camera, owners, local_block, connect):
    weights = shape_table()
    blocks = owners * BLK_DEV + local_block
    node_slots = MAXB * NBS
    steps_count = TILES // group_tiles

    def one_group(summed, inputs):
        pixels, cameras, block_ids, link_ids = inputs
        as_float = pixels.astype(jnp.float32)
        slope_x, slope_y = slopes(as_float)
        fetched = direction[block_ids]
        nodal_values = fetched.transpose(0, 2, 1, 3).reshape(group_tiles, 3, node_slots)
        projection = calibration[cameras]
        partial_sums = tile_terms(to_elements(slope_x), to_elements(slope_y), projection, nodal_values, link_ids, weights)
        partial_sums = partial_sums.reshape(group_tiles, 3, MAXB, NBS).transpose(0, 2, 1, 3).reshape(group_tiles * MAXB, 3, NBS)
        return summed.at[block_ids.reshape(-1)].add(partial_sums), None

    inputs = (images.reshape(steps_count, group_tiles, TPX, TPX), camera.reshape(steps_count, group_tiles), blocks.reshape(steps_count, group_tiles, MAXB), connect.reshape(steps_count, group_tiles, 4, ELEMS))
    summed, unused = lax.scan(one_group, jnp.zeros(direction.shape, jnp.float32), inputs)
    return summed + damping * direction
```

```python
import functools

import jax
import jax.numpy as jnp
import numpy as np
from jax import lax
from jax.experimental import pallas as pl
from jax.experimental.pallas import tpu as pltpu
from jax.sharding import PartitionSpec as P

EPX = 4
LANES = 128
SUBS = 8
AXES = ("tiles", "nodes")
VMEM_LIMIT = 48 * 1024 * 1024


def pair_weights():
    x = (np.arange(EPX, dtype=np.float64) + 0.5) / EPX
    return np.stack([(1 - x) ** 2, x * (1 - x), x**2])


def column_pool(width):
    cells = width // EPX
    groups = LANES // cells
    weights = pair_weights()
    table = np.zeros((groups, width, 3, groups, cells), np.float32)
    for group in range(groups):
        for pixel in range(width):
            table[group, pixel, :, group, pixel // EPX] = weights[:, pixel % EPX]
    return table.reshape(groups * width, 3 * LANES)


def pixel_kernel(images_ref, pool_ref, out_ref, padded, pooled, *, tiles_step, groups):
    weights = pair_weights()
    height = images_ref.shape[1]
    width = images_ref.shape[2]
    stride = EPX * groups
    lane = lax.broadcasted_iota(jnp.int32, (SUBS, width), 1)
    first = lane == 0
    last = lane == width - 1
    scale = jnp.where(first | last, 1.0, 0.5).astype(jnp.float32)
    for tile in range(tiles_step):
        pixels = images_ref[tile].astype(jnp.float32)
        padded[pl.ds(SUBS, height), :] = pixels
        padded[pl.ds(SUBS - 1, 1), :] = 2.0 * pixels[0:1] - pixels[1:2]
        padded[pl.ds(SUBS + height, 1), :] = 2.0 * pixels[height - 1 :] - pixels[height - 2 : height - 1]
        for group in range(groups):
            sums = [[None] * 3 for _ in range(3)]
            rows = [
                padded[pl.ds(SUBS + group * EPX + step, SUBS, stride=stride), :]
                for step in range(-1, EPX + 1)
            ]
            for step in range(EPX):
                here = rows[step + 1]
                slope_y = 0.5 * (rows[step + 2] - rows[step])
                left = jnp.where(first, here, pltpu.roll(here, 1, 1))
                right = jnp.where(last, here, pltpu.roll(here, width - 1, 1))
                slope_x = scale * (right - left)
                products = (slope_x * slope_x, slope_x * slope_y, slope_y * slope_y)
                for kind in range(3):
                    for pair in range(3):
                        term = float(weights[pair, step]) * products[kind]
                        old = sums[kind][pair]
                        sums[kind][pair] = term if old is None else old + term
            for kind in range(3):
                for pair in range(3):
                    row = (tile * 9 + kind * 3 + pair) * SUBS
                    pooled[pl.ds(row, SUBS), pl.ds(group * width, width)] = sums[kind][pair]
    values = pooled[...]
    high = values.astype(jnp.bfloat16)
    low = (values - high.astype(jnp.float32)).astype(jnp.bfloat16)
    pool = pool_ref[...]
    out_ref[...] = jnp.dot(high, pool, preferred_element_type=jnp.float32) + jnp.dot(
        low, pool, preferred_element_type=jnp.float32
    )


def pixel_sums(images):
    tiles, height, width = images.shape
    groups = LANES * EPX // width
    tiles_step = 4
    rows = tiles_step * 9 * SUBS
    pool = jnp.asarray(column_pool(width), jnp.bfloat16)
    return pl.pallas_call(
        functools.partial(pixel_kernel, tiles_step=tiles_step, groups=groups),
        grid=(tiles // tiles_step,),
        in_specs=[
            pl.BlockSpec((tiles_step, height, width), lambda i: (i, 0, 0)),
            pl.BlockSpec(pool.shape, lambda i: (0, 0)),
        ],
        out_specs=pl.BlockSpec((rows, 3 * LANES), lambda i: (i, 0)),
        out_shape=jax.ShapeDtypeStruct((tiles * 9 * SUBS, 3 * LANES), jnp.float32),
        scratch_shapes=[
            pltpu.VMEM((height + 2 * SUBS, width), jnp.float32),
            pltpu.VMEM((rows, groups * width), jnp.float32),
        ],
        compiler_params=pltpu.CompilerParams(vmem_limit_bytes=VMEM_LIMIT),
        cost_estimate=pl.CostEstimate(
            flops=tiles * 2 * 72 * 512 * 384 * 4, bytes_accessed=4 * images.size, transcendentals=0
        ),
        name="pixel_sums",
    )(images, pool)


def serve_kernel(codes_ref, calibration_ref, direction_ref, out_ref, table, *, capacity, devices):
    blocks = direction_ref.shape[1]
    cameras = calibration_ref.shape[0] // 6
    parts = [direction_ref[axis] for axis in range(3)]
    for camera in range(cameras):
        for motion in range(2):
            base = camera * 6 + motion * 3
            seen = calibration_ref[base] * parts[0]
            seen = seen + calibration_ref[base + 1] * parts[1]
            seen = seen + calibration_ref[base + 2] * parts[2]
            table[pl.ds((motion * cameras + camera) * blocks, blocks), :] = seen

    def one_device(device, carry):
        for slot in range(capacity):
            code = jnp.maximum(codes_ref[device * capacity + slot], 0)
            for motion in range(2):
                row = device * (2 * capacity) + motion * capacity + slot
                out_ref[pl.ds(row, 1), :] = table[pl.ds(motion * cameras * blocks + code, 1), :]
        return carry

    lax.fori_loop(0, devices, one_device, 0)


def serve(codes, calibration, direction, capacity, devices):
    _, blocks, width = direction.shape
    cameras = calibration.shape[0]
    return pl.pallas_call(
        functools.partial(serve_kernel, capacity=capacity, devices=devices),
        in_specs=[
            pl.BlockSpec(memory_space=pltpu.SMEM),
            pl.BlockSpec(memory_space=pltpu.SMEM),
            pl.BlockSpec(memory_space=pltpu.VMEM),
        ],
        out_specs=pl.BlockSpec(memory_space=pltpu.VMEM),
        out_shape=jax.ShapeDtypeStruct((devices * 2 * capacity, width), jnp.float32),
        scratch_shapes=[pltpu.VMEM((2 * cameras * blocks, width), jnp.float32)],
        compiler_params=pltpu.CompilerParams(vmem_limit_bytes=VMEM_LIMIT),
        name="serve",
    )(codes, calibration.reshape(-1), direction)


def tile_kernel(place_ref, arrived_ref, sums_ref, connect_ref, out_ref, result, *, capacity, listed):
    tile = pl.program_id(0)

    @pl.when(tile == 0)
    def _():
        out_ref[...] = jnp.zeros_like(out_ref)

    shape = (SUBS, LANES)
    node_of = []
    block_of = []
    motion = [[jnp.zeros(shape, jnp.float32) for _ in range(2)] for _ in range(4)]
    for corner in range(4):
        link = connect_ref[0, corner]
        node_of.append(jnp.bitwise_and(link, LANES - 1))
        block_of.append(jnp.right_shift(link, 7))
    for entry in range(listed):
        place = place_ref[tile * listed + entry]
        rows = [
            jnp.broadcast_to(arrived_ref[pl.ds(place + axis * capacity, 1), :], shape) for axis in range(2)
        ]
        for corner in range(4):
            here = block_of[corner] == entry
            for axis in range(2):
                picked = jnp.take_along_axis(rows[axis], node_of[corner], axis=1, mode="promise_in_bounds")
                motion[corner][axis] = jnp.where(here, picked, motion[corner][axis])

    def element(kind, pair_y, pair_x):
        return sums_ref[pl.ds((kind * 3 + pair_y) * SUBS, SUBS), pl.ds(pair_x * LANES, LANES)]

    forces = []
    for corner in range(4):
        both = []
        for axis in range(2):
            total = None
            for other in range(4):
                pair_x = corner % 2 + other % 2
                pair_y = corner // 2 + other // 2
                for source in range(2):
                    term = element(axis + source, pair_y, pair_x) * motion[other][source]
                    total = term if total is None else total + term
            both.append(total)
        forces.append(both)

    node_ids = lax.broadcasted_iota(jnp.int32, (LANES, LANES), 0)
    block_ids = lax.broadcasted_iota(jnp.int32, (listed, LANES), 0)
    total = jnp.zeros((4 * listed, LANES), jnp.float32)
    for corner in range(4):
        hots = []
        spreads = []
        split = []
        for axis in range(2):
            high = forces[corner][axis].astype(jnp.bfloat16).astype(jnp.float32)
            split += [high, forces[corner][axis] - high]
        for chunk in range(SUBS):
            nodes = jnp.broadcast_to(node_of[corner][chunk : chunk + 1], (LANES, LANES))
            hots.append(jnp.where(nodes == node_ids, 1.0, 0.0).astype(jnp.bfloat16))
            here = jnp.broadcast_to(block_of[corner][chunk : chunk + 1], (listed, LANES)) == block_ids
            spreads.append(
                jnp.concatenate(
                    [
                        jnp.where(here, jnp.broadcast_to(part[chunk : chunk + 1], (listed, LANES)), 0.0).astype(
                            jnp.bfloat16
                        )
                        for part in split
                    ],
                    axis=0,
                )
            )
        hot = jnp.concatenate(hots, axis=1)
        spread = jnp.concatenate(spreads, axis=1)
        total = total + lax.dot_general(
            spread, hot, (((1,), (1,)), ((), ())), preferred_element_type=jnp.float32
        )
    for axis in range(2):
        base = 2 * axis * listed
        result[pl.ds(axis * listed, listed), :] = (
            total[base : base + listed] + total[base + listed : base + 2 * listed]
        )
    for entry in range(listed):
        place = place_ref[tile * listed + entry]
        for axis in range(2):
            out_ref[pl.ds(place + axis * capacity, 1), :] = result[pl.ds(axis * listed + entry, 1), :]


def tile_forces(places, arrived, sums, connect, capacity, listed):
    tiles = connect.shape[0]
    return pl.pallas_call(
        functools.partial(tile_kernel, capacity=capacity, listed=listed),
        grid_spec=pltpu.PrefetchScalarGridSpec(
            num_scalar_prefetch=1,
            grid=(tiles,),
            in_specs=[
                pl.BlockSpec(arrived.shape, lambda i, *_: (0, 0)),
                pl.BlockSpec((9 * SUBS, 3 * LANES), lambda i, *_: (i, 0)),
                pl.BlockSpec((1, 4, SUBS, LANES), lambda i, *_: (i, 0, 0, 0)),
            ],
            out_specs=pl.BlockSpec(arrived.shape, lambda i, *_: (0, 0)),
            scratch_shapes=[pltpu.VMEM((2 * listed, LANES), jnp.float32)],
        ),
        out_shape=jax.ShapeDtypeStruct(arrived.shape, jnp.float32),
        compiler_params=pltpu.CompilerParams(vmem_limit_bytes=VMEM_LIMIT),
        name="tile_forces",
    )(places, arrived, sums, connect)


def finish_kernel(calibration_ref, codes_ref, back_ref, direction_ref, damping_ref, out_ref, *, capacity, devices):
    blocks = direction_ref.shape[1]
    cameras = calibration_ref.shape[0] // 6
    slots = devices * capacity
    back = back_ref[...].reshape(devices, 2, capacity, LANES)
    halves = []
    for motion in range(2):
        values = back[:, motion].reshape(slots, LANES)
        high = values.astype(jnp.bfloat16)
        halves += [high, (values - high.astype(jnp.float32)).astype(jnp.bfloat16)]
    right = jnp.concatenate(halves, axis=1)
    ids = lax.broadcasted_iota(jnp.int32, (cameras * blocks, LANES), 0)
    hot = jnp.concatenate(
        [
            jnp.where(
                jnp.broadcast_to(codes_ref[pl.ds(part, 1), :], ids.shape) == ids, 1.0, 0.0
            ).astype(jnp.bfloat16)
            for part in range(slots // LANES)
        ],
        axis=1,
    )
    summed = jnp.dot(hot, right, preferred_element_type=jnp.float32)
    seen = [
        summed[:, 2 * motion * LANES : (2 * motion + 1) * LANES]
        + summed[:, (2 * motion + 1) * LANES : (2 * motion + 2) * LANES]
        for motion in range(2)
    ]
    for axis in range(3):
        total = damping_ref[axis] * direction_ref[axis]
        for camera in range(cameras):
            for motion in range(2):
                part = seen[motion][camera * blocks : (camera + 1) * blocks]
                total = total + calibration_ref[camera * 6 + motion * 3 + axis] * part
        out_ref[axis] = total


def finish(calibration, codes, back, direction, damping, capacity, devices):
    vmem = pl.BlockSpec(memory_space=pltpu.VMEM)
    return pl.pallas_call(
        functools.partial(finish_kernel, capacity=capacity, devices=devices),
        in_specs=[pl.BlockSpec(memory_space=pltpu.SMEM), vmem, vmem, vmem, vmem],
        out_specs=vmem,
        out_shape=jax.ShapeDtypeStruct(direction.shape, jnp.float32),
        compiler_params=pltpu.CompilerParams(vmem_limit_bytes=VMEM_LIMIT),
        name="finish",
    )(calibration.reshape(-1), codes, back, direction, damping)


def exchange(values):
    return lax.all_to_all(values, AXES, split_axis=0, concat_axis=0, tiled=True)


def per_device(images, direction, damping, calibration, camera, owners, local_block, connect):
    devices = lax.axis_size(AXES)
    tiles, listed = owners.shape
    blocks, _, width = direction.shape
    capacity = max(2, min(tiles, 4 * tiles * listed // devices))
    direction = direction.transpose(1, 0, 2)
    damping = damping.transpose(1, 0, 2)
    everyone = jnp.arange(devices, dtype=jnp.int32)
    code = camera[:, None] * blocks + local_block
    hits = owners[None, :, :] == everyone[:, None, None]
    named = jnp.sum(jnp.where(hits, code[None] + 1, 0), axis=2)
    if capacity == tiles:
        wanted = named - 1
        slot = jnp.broadcast_to(jnp.arange(tiles, dtype=jnp.int32)[:, None], owners.shape)
    else:
        taken = (named > 0).astype(jnp.int32)
        rank = jnp.cumsum(taken, axis=1) - taken
        slots = jnp.arange(capacity, dtype=jnp.int32)
        chosen = (rank[:, :, None] == slots[None, None, :]) & (taken[:, :, None] > 0)
        wanted = jnp.sum(jnp.where(chosen, named[:, :, None], 0), axis=1) - 1
        slot = jnp.sum(jnp.where(hits, rank[:, :, None], 0), axis=0)
    places = (owners * (2 * capacity) + slot).reshape(-1)
    asked = exchange(wanted).reshape(-1)
    sums = pixel_sums(images)
    outgoing = serve(asked, calibration, direction, capacity, devices)
    shape = (devices, 2 * capacity, width)
    arrived = exchange(outgoing.reshape(shape)).reshape(-1, width)
    forces = tile_forces(places, arrived, sums, connect.reshape(tiles, 4, SUBS, LANES), capacity, listed)
    back = exchange(forces.reshape(shape)).reshape(-1, width)
    product = finish(calibration, asked.reshape(-1, LANES), back, direction, damping, capacity, devices)
    return product.transpose(1, 0, 2)


def solution(mesh):
    split = P(AXES)
    return jax.shard_map(
        per_device,
        mesh=mesh,
        in_specs=(split, split, split, P(), split, split, split, split),
        out_specs=split,
        check_vma=False,
    )
```

```python
import functools
import math

import jax
import jax.numpy as jnp
import numpy as np
from jax import lax
from jax.experimental import pallas as pl
from jax.experimental.pallas import tpu as pltpu
from jax.sharding import PartitionSpec as P

EPX = 4
LANES = 128
SUBS = 8
AXES = ("tiles", "nodes")
VMEM_LIMIT = 48 * 1024 * 1024


def pair_weights():
    x = (np.arange(EPX, dtype=np.float64) + 0.5) / EPX
    return np.stack([(1 - x) ** 2, x * (1 - x), x**2])


def column_pool(width):
    cells = width // EPX
    groups = LANES // cells
    weights = pair_weights()
    table = np.zeros((groups, width, 3, groups, cells), np.float32)
    for group in range(groups):
        for pixel in range(width):
            table[group, pixel, :, group, pixel // EPX] = weights[:, pixel % EPX]
    return table.reshape(groups * width, 3 * LANES)


def pixel_kernel(images_ref, pool_ref, out_ref, padded, pooled, *, tiles_step, groups):
    weights = pair_weights()
    height = images_ref.shape[1]
    width = images_ref.shape[2]
    stride = EPX * groups
    lane = lax.broadcasted_iota(jnp.int32, (SUBS, width), 1)
    first = lane == 0
    last = lane == width - 1
    scale = jnp.where(first | last, 1.0, 0.5).astype(jnp.float32)
    for tile in range(tiles_step):
        pixels = images_ref[tile].astype(jnp.float32)
        padded[pl.ds(SUBS, height), :] = pixels
        padded[pl.ds(SUBS - 1, 1), :] = 2.0 * pixels[0:1] - pixels[1:2]
        padded[pl.ds(SUBS + height, 1), :] = 2.0 * pixels[height - 1 :] - pixels[height - 2 : height - 1]
        for group in range(groups):
            sums = [[None] * 3 for _ in range(3)]
            rows = [
                padded[pl.ds(SUBS + group * EPX + step, SUBS, stride=stride), :]
                for step in range(-1, EPX + 1)
            ]
            for step in range(EPX):
                here = rows[step + 1]
                slope_y = 0.5 * (rows[step + 2] - rows[step])
                left = jnp.where(first, here, pltpu.roll(here, 1, 1))
                right = jnp.where(last, here, pltpu.roll(here, width - 1, 1))
                slope_x = scale * (right - left)
                products = (slope_x * slope_x, slope_x * slope_y, slope_y * slope_y)
                for kind in range(3):
                    for pair in range(3):
                        term = float(weights[pair, step]) * products[kind]
                        old = sums[kind][pair]
                        sums[kind][pair] = term if old is None else old + term
            for kind in range(3):
                for pair in range(3):
                    row = (tile * 9 + kind * 3 + pair) * SUBS
                    pooled[pl.ds(row, SUBS), pl.ds(group * width, width)] = sums[kind][pair]
    values = pooled[...]
    high = values.astype(jnp.bfloat16)
    low = (values - high.astype(jnp.float32)).astype(jnp.bfloat16)
    pool = pool_ref[...]
    out_ref[...] = jnp.dot(high, pool, preferred_element_type=jnp.float32) + jnp.dot(
        low, pool, preferred_element_type=jnp.float32
    )


def pixel_sums(images):
    tiles, height, width = images.shape
    groups = LANES * EPX // width
    tiles_step = 4
    rows = tiles_step * 9 * SUBS
    pool = jnp.asarray(column_pool(width), jnp.bfloat16)
    return pl.pallas_call(
        functools.partial(pixel_kernel, tiles_step=tiles_step, groups=groups),
        grid=(tiles // tiles_step,),
        in_specs=[
            pl.BlockSpec((tiles_step, height, width), lambda i: (i, 0, 0)),
            pl.BlockSpec(pool.shape, lambda i: (0, 0)),
        ],
        out_specs=pl.BlockSpec((rows, 3 * LANES), lambda i: (i, 0)),
        out_shape=jax.ShapeDtypeStruct((tiles * 9 * SUBS, 3 * LANES), jnp.float32),
        scratch_shapes=[
            pltpu.VMEM((height + 2 * SUBS, width), jnp.float32),
            pltpu.VMEM((rows, groups * width), jnp.float32),
        ],
        compiler_params=pltpu.CompilerParams(vmem_limit_bytes=VMEM_LIMIT),
        cost_estimate=pl.CostEstimate(
            flops=tiles * 2 * 72 * 512 * 384 * 4, bytes_accessed=4 * images.size, transcendentals=0
        ),
        name="pixel_sums",
    )(images, pool)


def table_kernel(calibration_ref, direction_ref, out_ref):
    blocks = direction_ref.shape[1]
    cameras = calibration_ref.shape[0] // 6
    parts = [direction_ref[axis] for axis in range(3)]
    for camera in range(cameras):
        for motion in range(2):
            base = camera * 6 + motion * 3
            seen = calibration_ref[base] * parts[0]
            seen = seen + calibration_ref[base + 1] * parts[1]
            seen = seen + calibration_ref[base + 2] * parts[2]
            out_ref[pl.ds((motion * cameras + camera) * blocks, blocks), :] = seen


def seen_table(calibration, direction):
    _, blocks, width = direction.shape
    cameras = calibration.shape[0] // 6
    return pl.pallas_call(
        table_kernel,
        in_specs=[pl.BlockSpec(memory_space=pltpu.SMEM), pl.BlockSpec(memory_space=pltpu.VMEM)],
        out_specs=pl.BlockSpec(memory_space=pltpu.VMEM),
        out_shape=jax.ShapeDtypeStruct((2 * cameras * blocks, width), jnp.float32),
        compiler_params=pltpu.CompilerParams(vmem_limit_bytes=VMEM_LIMIT),
        cost_estimate=pl.CostEstimate(flops=10**6, bytes_accessed=2 * direction.size, transcendentals=0),
        name="seen_table",
    )(calibration, direction)


def serve_kernel(codes_ref, table_ref, out_ref):
    devices, capacity = codes_ref.shape
    half = table_ref.shape[0] // 2

    def one_device(device, carry):
        base = pl.multiple_of(device * (2 * capacity), 2 * capacity)
        for slot in range(capacity):
            code = jnp.maximum(codes_ref[device, slot], 0)
            for motion in range(2):
                out_ref[pl.ds(base + motion * capacity + slot, 1), :] = table_ref[
                    pl.ds(motion * half + code, 1), :
                ]
        return carry

    lax.fori_loop(0, devices, one_device, 0, unroll=4)


def serve(codes, table):
    devices, capacity = codes.shape
    return pl.pallas_call(
        serve_kernel,
        in_specs=[pl.BlockSpec(memory_space=pltpu.SMEM), pl.BlockSpec(memory_space=pltpu.VMEM)],
        out_specs=pl.BlockSpec(memory_space=pltpu.VMEM),
        out_shape=jax.ShapeDtypeStruct((devices * 2 * capacity, table.shape[1]), jnp.float32),
        compiler_params=pltpu.CompilerParams(vmem_limit_bytes=VMEM_LIMIT),
        name="serve",
    )(codes, table)


def request_kernel(owners_ref, local_ref, camera_ref, out_ref, *, blocks):
    owners = owners_ref[...].T
    local = local_ref[...].T
    everyone = lax.broadcasted_iota(jnp.int32, out_ref.shape, 0)
    code = camera_ref[...] * blocks
    wanted = jnp.full(out_ref.shape, -1, jnp.int32)
    for entry in range(owners.shape[0]):
        here = jnp.broadcast_to(owners[entry : entry + 1], out_ref.shape) == everyone
        wanted = jnp.where(here, jnp.broadcast_to(code + local[entry : entry + 1], out_ref.shape), wanted)
    out_ref[...] = wanted


def requests(owners, local_block, camera, blocks, devices):
    vmem = pl.BlockSpec(memory_space=pltpu.VMEM)
    return pl.pallas_call(
        functools.partial(request_kernel, blocks=blocks),
        in_specs=[vmem, vmem, vmem],
        out_specs=vmem,
        out_shape=jax.ShapeDtypeStruct((devices, owners.shape[0]), jnp.int32),
        name="requests",
    )(owners, local_block, camera.reshape(1, -1))


def tile_kernel(place_ref, arrived_ref, sums_ref, connect_ref, out_ref, parts, result, *, capacity, listed, group):
    tiles = connect_ref.shape[0]
    shape = (SUBS, LANES)
    out_ref[...] = jnp.zeros_like(out_ref)

    def one_tile(tile, parts, result):
        links = [connect_ref[tile, corner] for corner in range(4)]
        node_of = [jnp.bitwise_and(link, LANES - 1) for link in links]
        block_of = [jnp.right_shift(link, 7) for link in links]
        motion = [[jnp.zeros(shape, jnp.float32) for _ in range(2)] for _ in range(4)]
        for entry in range(listed):
            place = place_ref[tile, entry]
            rows = [
                jnp.broadcast_to(arrived_ref[pl.ds(place + axis * capacity, 1), :], shape) for axis in range(2)
            ]
            for corner in range(4):
                here = block_of[corner] == entry
                for axis in range(2):
                    picked = jnp.take_along_axis(rows[axis], node_of[corner], axis=1, mode="promise_in_bounds")
                    motion[corner][axis] = jnp.where(here, picked, motion[corner][axis])

        def element(kind, pair_y, pair_x):
            row = pl.multiple_of(tile * (9 * SUBS), SUBS) + (kind * 3 + pair_y) * SUBS
            return sums_ref[pl.ds(row, SUBS), pl.ds(pair_x * LANES, LANES)]

        for corner in range(4):
            for axis in range(2):
                total = None
                for other in range(4):
                    pair_x = corner % 2 + other % 2
                    pair_y = corner // 2 + other // 2
                    for source in range(2):
                        term = element(axis + source, pair_y, pair_x) * motion[other][source]
                        total = term if total is None else total + term
                high = total.astype(jnp.bfloat16).astype(jnp.float32)
                row = (corner * 4 + axis * 2) * SUBS
                parts[pl.ds(row, SUBS), :] = high
                parts[pl.ds(row + SUBS, SUBS), :] = total - high

        node_ids = lax.broadcasted_iota(jnp.int32, (LANES, LANES), 0)
        block_ids = lax.broadcasted_iota(jnp.int32, (listed, LANES), 0)
        total = None
        for corner in range(4):
            hots = []
            spreads = []
            for chunk in range(SUBS):
                link = connect_ref[tile, corner, pl.ds(chunk, 1), :]
                nodes = jnp.broadcast_to(jnp.bitwise_and(link, LANES - 1), (LANES, LANES))
                hots.append(jnp.where(nodes == node_ids, 1.0, 0.0).astype(jnp.bfloat16))
                here = jnp.broadcast_to(jnp.right_shift(link, 7), (listed, LANES)) == block_ids
                chosen = []
                for part in range(4):
                    row = parts[pl.ds((corner * 4 + part) * SUBS + chunk, 1), :]
                    chosen.append(jnp.where(here, jnp.broadcast_to(row, (listed, LANES)), 0.0).astype(jnp.bfloat16))
                spreads.append(jnp.concatenate(chosen, axis=0))
            term = lax.dot_general(
                jnp.concatenate(spreads, axis=1),
                jnp.concatenate(hots, axis=1),
                (((1,), (1,)), ((), ())),
                preferred_element_type=jnp.float32,
            )
            total = term if total is None else total + term
        for axis in range(2):
            base = 2 * axis * listed
            result[pl.ds(axis * listed, listed), :] = (
                total[base : base + listed] + total[base + listed : base + 2 * listed]
            )
        for entry in range(listed):
            place = place_ref[tile, entry]
            for axis in range(2):
                out_ref[pl.ds(place + axis * capacity, 1), :] = result[pl.ds(axis * listed + entry, 1), :]

    def one_group(step, carry):
        for member in range(group):
            one_tile(step * group + member, parts.at[member], result.at[member])
        return carry

    lax.fori_loop(0, tiles // group, one_group, 0)


def tile_forces(places, arrived, sums, connect, capacity):
    tiles, listed = places.shape
    group = math.gcd(tiles, 8)
    vmem = pl.BlockSpec(memory_space=pltpu.VMEM)
    return pl.pallas_call(
        functools.partial(tile_kernel, capacity=capacity, listed=listed, group=group),
        in_specs=[pl.BlockSpec(memory_space=pltpu.SMEM), vmem, vmem, vmem],
        out_specs=vmem,
        out_shape=jax.ShapeDtypeStruct(arrived.shape, jnp.float32),
        scratch_shapes=[
            pltpu.VMEM((group, 16 * SUBS, LANES), jnp.float32),
            pltpu.VMEM((group, 2 * listed, LANES), jnp.float32),
        ],
        compiler_params=pltpu.CompilerParams(vmem_limit_bytes=VMEM_LIMIT),
        name="tile_forces",
    )(places, arrived, sums, connect)


def hot_kernel(codes_ref, direction_ref, damping_ref, hot_ref, damped_ref):
    for part in range(codes_ref.shape[0]):
        ids = lax.broadcasted_iota(jnp.int32, (hot_ref.shape[0], LANES), 0)
        here = jnp.broadcast_to(codes_ref[pl.ds(part, 1), :], ids.shape) == ids
        hot_ref[:, pl.ds(part * LANES, LANES)] = jnp.where(here, 1.0, 0.0).astype(jnp.bfloat16)
    damped_ref[...] = damping_ref[...] * direction_ref[...]


def hot_table(codes, direction, damping, cameras):
    vmem = pl.BlockSpec(memory_space=pltpu.VMEM)
    shape = (cameras * direction.shape[1], codes.size)
    return pl.pallas_call(
        hot_kernel,
        in_specs=[vmem, vmem, vmem],
        out_specs=(vmem, vmem),
        out_shape=(
            jax.ShapeDtypeStruct(shape, jnp.bfloat16),
            jax.ShapeDtypeStruct(direction.shape, jnp.float32),
        ),
        compiler_params=pltpu.CompilerParams(vmem_limit_bytes=VMEM_LIMIT),
        cost_estimate=pl.CostEstimate(flops=10**6, bytes_accessed=10**6, transcendentals=0),
        name="hot_table",
    )(codes, direction, damping)


def finish_kernel(calibration_ref, hot_ref, back_ref, damped_ref, out_ref, *, capacity, devices):
    blocks = damped_ref.shape[1]
    cameras = calibration_ref.shape[0] // 6
    slots = devices * capacity
    back = back_ref[...].reshape(devices, 2, capacity, LANES)
    halves = []
    for motion in range(2):
        values = back[:, motion].reshape(slots, LANES)
        high = values.astype(jnp.bfloat16)
        halves += [high, (values - high.astype(jnp.float32)).astype(jnp.bfloat16)]
    right = jnp.concatenate(halves, axis=1)
    totals = [damped_ref[axis] for axis in range(3)]
    for camera in range(cameras):
        summed = jnp.dot(
            hot_ref[pl.ds(camera * blocks, blocks), :], right, preferred_element_type=jnp.float32
        )
        for motion in range(2):
            base = 2 * motion * LANES
            seen = summed[:, base : base + LANES] + summed[:, base + LANES : base + 2 * LANES]
            for axis in range(3):
                totals[axis] = totals[axis] + calibration_ref[camera * 6 + motion * 3 + axis] * seen
    for axis in range(3):
        out_ref[axis] = totals[axis]


def finish(calibration, hot, back, damped, capacity, devices):
    vmem = pl.BlockSpec(memory_space=pltpu.VMEM)
    return pl.pallas_call(
        functools.partial(finish_kernel, capacity=capacity, devices=devices),
        in_specs=[pl.BlockSpec(memory_space=pltpu.SMEM), vmem, vmem, vmem],
        out_specs=vmem,
        out_shape=jax.ShapeDtypeStruct(damped.shape, jnp.float32),
        compiler_params=pltpu.CompilerParams(vmem_limit_bytes=VMEM_LIMIT),
        name="finish",
    )(calibration, hot, back, damped)


def exchange(values):
    return lax.all_to_all(values, AXES, split_axis=0, concat_axis=0, tiled=True)


def per_device(images, direction, damping, calibration, camera, owners, local_block, connect):
    devices = lax.axis_size(AXES)
    tiles, listed = owners.shape
    blocks, _, width = direction.shape
    cameras = calibration.shape[0]
    capacity = max(2, min(tiles, 4 * tiles * listed // devices))
    direction = direction.transpose(1, 0, 2)
    damping = damping.transpose(1, 0, 2)
    calibration = calibration.reshape(-1)
    if capacity == tiles:
        wanted = requests(owners, local_block, camera, blocks, devices)
        slot = jnp.broadcast_to(jnp.arange(tiles, dtype=jnp.int32)[:, None], owners.shape)
    else:
        everyone = jnp.arange(devices, dtype=jnp.int32)
        code = camera[:, None] * blocks + local_block
        hits = owners[None, :, :] == everyone[:, None, None]
        named = jnp.sum(jnp.where(hits, code[None] + 1, 0), axis=2)
        taken = (named > 0).astype(jnp.int32)
        rank = jnp.cumsum(taken, axis=1) - taken
        slots = jnp.arange(capacity, dtype=jnp.int32)
        chosen = (rank[:, :, None] == slots[None, None, :]) & (taken[:, :, None] > 0)
        wanted = jnp.sum(jnp.where(chosen, named[:, :, None], 0), axis=1) - 1
        slot = jnp.sum(jnp.where(hits, rank[:, :, None], 0), axis=0)
    places = owners * (2 * capacity) + slot
    asked = exchange(wanted.reshape(devices, 1, capacity)).reshape(devices, capacity)
    table = seen_table(calibration, direction)
    sums = pixel_sums(images)
    outgoing = serve(asked, table)
    shape = (devices, 2 * capacity, width)
    arrived = exchange(outgoing.reshape(shape)).reshape(-1, width)
    hot, damped = hot_table(asked.reshape(-1, LANES), direction, damping, cameras)
    forces = tile_forces(places, arrived, sums, connect.reshape(tiles, 4, SUBS, LANES), capacity)
    back = exchange(forces.reshape(shape)).reshape(-1, width)
    product = finish(calibration, hot, back, damped, capacity, devices)
    return product.transpose(1, 0, 2)


def solution(mesh):
    split = P(AXES)
    return jax.shard_map(
        per_device,
        mesh=mesh,
        in_specs=(split, split, split, P(), split, split, split, split),
        out_specs=split,
        check_vma=False,
    )
```

```python
import functools
import math

import jax
import jax.numpy as jnp
import numpy as np
from jax import lax
from jax.experimental import pallas as pl
from jax.experimental.pallas import tpu as pltpu
from jax.sharding import PartitionSpec as P

EPX = 4
LANES = 128
SUBS = 8
AXES = ("tiles", "nodes")
VMEM_LIMIT = 48 * 1024 * 1024


def pair_weights():
    x = (np.arange(EPX, dtype=np.float64) + 0.5) / EPX
    return np.stack([(1 - x) ** 2, x * (1 - x), x**2])


def column_pool(width):
    cells = width // EPX
    groups = LANES // cells
    weights = pair_weights()
    table = np.zeros((groups, width, 3, groups, cells), np.float32)
    for group in range(groups):
        for pixel in range(width):
            table[group, pixel, :, group, pixel // EPX] = weights[:, pixel % EPX]
    return table.reshape(groups * width, 3 * LANES)


def pixel_kernel(images_ref, pool_ref, out_ref, padded, pooled, *, tiles_step, groups):
    weights = pair_weights()
    height = images_ref.shape[1]
    width = images_ref.shape[2]
    stride = EPX * groups
    lane = lax.broadcasted_iota(jnp.int32, (SUBS, width), 1)
    first = lane == 0
    last = lane == width - 1
    scale = jnp.where(first | last, 1.0, 0.5).astype(jnp.float32)
    for tile in range(tiles_step):
        pixels = images_ref[tile].astype(jnp.float32)
        padded[pl.ds(SUBS, height), :] = pixels
        padded[pl.ds(SUBS - 1, 1), :] = 2.0 * pixels[0:1] - pixels[1:2]
        padded[pl.ds(SUBS + height, 1), :] = 2.0 * pixels[height - 1 :] - pixels[height - 2 : height - 1]
        for group in range(groups):
            sums = [[None] * 3 for _ in range(3)]
            rows = [
                padded[pl.ds(SUBS + group * EPX + step, SUBS, stride=stride), :]
                for step in range(-1, EPX + 1)
            ]
            for step in range(EPX):
                here = rows[step + 1]
                slope_y = 0.5 * (rows[step + 2] - rows[step])
                left = jnp.where(first, here, pltpu.roll(here, 1, 1))
                right = jnp.where(last, here, pltpu.roll(here, width - 1, 1))
                slope_x = scale * (right - left)
                products = (slope_x * slope_x, slope_x * slope_y, slope_y * slope_y)
                for kind in range(3):
                    for pair in range(3):
                        term = float(weights[pair, step]) * products[kind]
                        old = sums[kind][pair]
                        sums[kind][pair] = term if old is None else old + term
            for kind in range(3):
                for pair in range(3):
                    row = (tile * 9 + kind * 3 + pair) * SUBS
                    pooled[pl.ds(row, SUBS), pl.ds(group * width, width)] = sums[kind][pair]
    values = pooled[...]
    high = values.astype(jnp.bfloat16)
    low = (values - high.astype(jnp.float32)).astype(jnp.bfloat16)
    pool = pool_ref[...]
    out_ref[...] = jnp.dot(high, pool, preferred_element_type=jnp.float32) + jnp.dot(
        low, pool, preferred_element_type=jnp.float32
    )


def pixel_sums(images):
    tiles, height, width = images.shape
    groups = LANES * EPX // width
    tiles_step = 4
    rows = tiles_step * 9 * SUBS
    pool = jnp.asarray(column_pool(width), jnp.bfloat16)
    return pl.pallas_call(
        functools.partial(pixel_kernel, tiles_step=tiles_step, groups=groups),
        grid=(tiles // tiles_step,),
        in_specs=[
            pl.BlockSpec((tiles_step, height, width), lambda i: (i, 0, 0)),
            pl.BlockSpec(pool.shape, lambda i: (0, 0)),
        ],
        out_specs=pl.BlockSpec((rows, 3 * LANES), lambda i: (i, 0)),
        out_shape=jax.ShapeDtypeStruct((tiles * 9 * SUBS, 3 * LANES), jnp.float32),
        scratch_shapes=[
            pltpu.VMEM((height + 2 * SUBS, width), jnp.float32),
            pltpu.VMEM((rows, groups * width), jnp.float32),
        ],
        compiler_params=pltpu.CompilerParams(vmem_limit_bytes=VMEM_LIMIT),
        cost_estimate=pl.CostEstimate(
            flops=tiles * 2 * 72 * 512 * 384 * 4, bytes_accessed=4 * images.size, transcendentals=0
        ),
        name="pixel_sums",
    )(images, pool)


def table_kernel(calibration_ref, direction_ref, out_ref):
    blocks = direction_ref.shape[1]
    cameras = calibration_ref.shape[0] // 6
    half = cameras * blocks
    parts = [direction_ref[axis] for axis in range(3)]
    for camera in range(cameras):
        for motion in range(2):
            base = camera * 6 + motion * 3
            seen = calibration_ref[base] * parts[0]
            seen = seen + calibration_ref[base + 1] * parts[1]
            seen = seen + calibration_ref[base + 2] * parts[2]
            out_ref[pl.ds(motion * half + camera * blocks, blocks), :] = seen
    out_ref[pl.ds(2 * half, 2 * SUBS), :] = jnp.zeros((2 * SUBS, out_ref.shape[1]), jnp.float32)


def seen_table(calibration, direction):
    _, blocks, width = direction.shape
    cameras = calibration.shape[0] // 6
    return pl.pallas_call(
        table_kernel,
        in_specs=[pl.BlockSpec(memory_space=pltpu.SMEM), pl.BlockSpec(memory_space=pltpu.VMEM)],
        out_specs=pl.BlockSpec(memory_space=pltpu.VMEM),
        out_shape=jax.ShapeDtypeStruct((2 * (cameras * blocks + SUBS), width), jnp.float32),
        compiler_params=pltpu.CompilerParams(vmem_limit_bytes=VMEM_LIMIT),
        cost_estimate=pl.CostEstimate(flops=10**6, bytes_accessed=2 * direction.size, transcendentals=0),
        name="seen_table",
    )(calibration, direction)


def serve_kernel(codes_ref, table_ref, out_ref, rows, sems, *, capacity):
    devices = codes_ref.shape[0] // capacity
    half = table_ref.shape[0] // 2 - SUBS
    pieces = sems.shape[0]
    length = rows.shape[0] // pieces
    copies = []
    for piece in range(pieces):
        for device in range(piece * devices // pieces, (piece + 1) * devices // pieces):
            for slot in range(capacity):
                code = codes_ref[device * capacity + slot]
                for motion in range(2):
                    row = device * (2 * capacity) + motion * capacity + slot
                    rows[pl.ds(row, 1), :] = table_ref[pl.ds(motion * half + code, 1), :]
        place = pl.ds(piece * length, length)
        copies.append(pltpu.make_async_copy(rows.at[place], out_ref.at[place], sems.at[piece]))
        copies[-1].start()
    for copy in copies:
        copy.wait()


def serve(codes, table):
    devices, capacity = codes.shape
    shape = (devices * 2 * capacity, table.shape[1])
    return pl.pallas_call(
        functools.partial(serve_kernel, capacity=capacity),
        in_specs=[pl.BlockSpec(memory_space=pltpu.SMEM), pl.BlockSpec(memory_space=pltpu.VMEM)],
        out_specs=pl.BlockSpec(memory_space=pl.ANY),
        out_shape=jax.ShapeDtypeStruct(shape, jnp.float32),
        scratch_shapes=[pltpu.VMEM(shape, jnp.float32), pltpu.SemaphoreType.DMA((math.gcd(devices, 8),))],
        compiler_params=pltpu.CompilerParams(vmem_limit_bytes=VMEM_LIMIT),
        name="serve",
    )(codes.reshape(-1), table)


def request_kernel(owners_ref, local_ref, camera_ref, out_ref, *, blocks, nothing):
    owners = owners_ref[...].T
    local = local_ref[...].T
    everyone = lax.broadcasted_iota(jnp.int32, out_ref.shape, 0)
    code = camera_ref[...] * blocks
    wanted = jnp.full(out_ref.shape, nothing, jnp.int32)
    for entry in range(owners.shape[0]):
        here = jnp.broadcast_to(owners[entry : entry + 1], out_ref.shape) == everyone
        wanted = jnp.where(here, jnp.broadcast_to(code + local[entry : entry + 1], out_ref.shape), wanted)
    out_ref[...] = wanted


def requests(owners, local_block, camera, blocks, devices, nothing):
    vmem = pl.BlockSpec(memory_space=pltpu.VMEM)
    return pl.pallas_call(
        functools.partial(request_kernel, blocks=blocks, nothing=nothing),
        in_specs=[vmem, vmem, vmem],
        out_specs=vmem,
        out_shape=jax.ShapeDtypeStruct((devices, owners.shape[0]), jnp.int32),
        name="requests",
    )(owners, local_block, camera.reshape(1, -1))


def tile_kernel(place_ref, arrived_ref, sums_ref, connect_ref, out_ref, parts, result, *, capacity, listed, group):
    tiles = connect_ref.shape[0]
    shape = (SUBS, LANES)
    out_ref[...] = jnp.zeros_like(out_ref)

    def one_tile(tile, parts, result):
        links = [connect_ref[tile, corner] for corner in range(4)]
        node_of = [jnp.bitwise_and(link, LANES - 1) for link in links]
        block_of = [jnp.right_shift(link, 7) for link in links]
        motion = [[jnp.zeros(shape, jnp.float32) for _ in range(2)] for _ in range(4)]
        places = [place_ref[tile * listed + entry] for entry in range(listed)]
        for corner in range(4):
            for axis in range(2):
                for entry in range(listed):
                    row = arrived_ref[pl.ds(places[entry] + axis * capacity, 1), :]
                    picked = jnp.take_along_axis(
                        jnp.broadcast_to(row, shape), node_of[corner], axis=1, mode="promise_in_bounds"
                    )
                    motion[corner][axis] = jnp.where(block_of[corner] == entry, picked, motion[corner][axis])

        def element(kind, pair_y, pair_x):
            row = pl.multiple_of(tile * (9 * SUBS), SUBS) + (kind * 3 + pair_y) * SUBS
            return sums_ref[pl.ds(row, SUBS), pl.ds(pair_x * LANES, LANES)]

        for corner in range(4):
            for axis in range(2):
                total = None
                for other in range(4):
                    pair_x = corner % 2 + other % 2
                    pair_y = corner // 2 + other // 2
                    for source in range(2):
                        term = element(axis + source, pair_y, pair_x) * motion[other][source]
                        total = term if total is None else total + term
                high = total.astype(jnp.bfloat16).astype(jnp.float32)
                row = (corner * 4 + axis * 2) * SUBS
                parts[pl.ds(row, SUBS), :] = high
                parts[pl.ds(row + SUBS, SUBS), :] = total - high

        node_ids = lax.broadcasted_iota(jnp.int32, (LANES, LANES), 0)
        block_ids = lax.broadcasted_iota(jnp.int32, (listed, LANES), 0)
        total = None
        for corner in range(4):
            hots = []
            spreads = []
            for chunk in range(SUBS):
                link = connect_ref[tile, corner, pl.ds(chunk, 1), :]
                nodes = jnp.broadcast_to(jnp.bitwise_and(link, LANES - 1), (LANES, LANES))
                hots.append(jnp.where(nodes == node_ids, 1.0, 0.0).astype(jnp.bfloat16))
                here = jnp.broadcast_to(jnp.right_shift(link, 7), (listed, LANES)) == block_ids
                chosen = []
                for part in range(4):
                    row = parts[pl.ds((corner * 4 + part) * SUBS + chunk, 1), :]
                    chosen.append(jnp.where(here, jnp.broadcast_to(row, (listed, LANES)), 0.0).astype(jnp.bfloat16))
                spreads.append(jnp.concatenate(chosen, axis=0))
            term = lax.dot_general(
                jnp.concatenate(spreads, axis=1),
                jnp.concatenate(hots, axis=1),
                (((1,), (1,)), ((), ())),
                preferred_element_type=jnp.float32,
            )
            total = term if total is None else total + term
        for axis in range(2):
            base = 2 * axis * listed
            result[pl.ds(axis * listed, listed), :] = (
                total[base : base + listed] + total[base + listed : base + 2 * listed]
            )
        for entry in range(listed):
            for axis in range(2):
                out_ref[pl.ds(places[entry] + axis * capacity, 1), :] = result[pl.ds(axis * listed + entry, 1), :]

    def one_group(step, carry):
        for member in range(group):
            one_tile(step * group + member, parts.at[member], result.at[member])
        return carry

    lax.fori_loop(0, tiles // group, one_group, 0)


def tile_forces(places, arrived, sums, connect, capacity):
    tiles, listed = places.shape
    group = math.gcd(tiles, 16)
    vmem = pl.BlockSpec(memory_space=pltpu.VMEM)
    return pl.pallas_call(
        functools.partial(tile_kernel, capacity=capacity, listed=listed, group=group),
        in_specs=[pl.BlockSpec(memory_space=pltpu.SMEM), vmem, vmem, vmem],
        out_specs=vmem,
        out_shape=jax.ShapeDtypeStruct(arrived.shape, jnp.float32),
        scratch_shapes=[
            pltpu.VMEM((group, 16 * SUBS, LANES), jnp.float32),
            pltpu.VMEM((group, 2 * listed, LANES), jnp.float32),
        ],
        compiler_params=pltpu.CompilerParams(vmem_limit_bytes=VMEM_LIMIT),
        name="tile_forces",
    )(places.reshape(-1), arrived, sums, connect)


def hot_kernel(codes_ref, direction_ref, damping_ref, hot_ref, damped_ref):
    for part in range(codes_ref.shape[0]):
        ids = lax.broadcasted_iota(jnp.int32, (hot_ref.shape[0], LANES), 0)
        here = jnp.broadcast_to(codes_ref[pl.ds(part, 1), :], ids.shape) == ids
        hot_ref[:, pl.ds(part * LANES, LANES)] = jnp.where(here, 1.0, 0.0).astype(jnp.bfloat16)
    damped_ref[...] = damping_ref[...] * direction_ref[...]


def hot_table(codes, direction, damping, cameras):
    vmem = pl.BlockSpec(memory_space=pltpu.VMEM)
    shape = (cameras * direction.shape[1], codes.size)
    return pl.pallas_call(
        hot_kernel,
        in_specs=[vmem, vmem, vmem],
        out_specs=(vmem, vmem),
        out_shape=(
            jax.ShapeDtypeStruct(shape, jnp.bfloat16),
            jax.ShapeDtypeStruct(direction.shape, jnp.float32),
        ),
        compiler_params=pltpu.CompilerParams(vmem_limit_bytes=VMEM_LIMIT),
        cost_estimate=pl.CostEstimate(flops=10**6, bytes_accessed=10**6, transcendentals=0),
        name="hot_table",
    )(codes, direction, damping)


def finish_kernel(calibration_ref, hot_ref, back_ref, damped_ref, out_ref, rows, sems, *, capacity, devices):
    blocks = damped_ref.shape[1]
    cameras = calibration_ref.shape[0] // 6
    slots = devices * capacity
    back = back_ref[...].reshape(devices, 2, capacity, LANES)
    halves = []
    for motion in range(2):
        values = back[:, motion].reshape(slots, LANES)
        high = values.astype(jnp.bfloat16)
        halves += [high, (values - high.astype(jnp.float32)).astype(jnp.bfloat16)]
    right = jnp.concatenate(halves, axis=1)
    summed = jnp.dot(hot_ref[...], right, preferred_element_type=jnp.float32)
    seen = []
    for motion in range(2):
        base = 2 * motion * LANES
        seen.append(summed[:, base : base + LANES] + summed[:, base + LANES : base + 2 * LANES])
    copies = []
    for axis in range(3):
        total = damped_ref[axis]
        for camera in range(cameras):
            for motion in range(2):
                factor = calibration_ref[pl.ds(camera * 6 + motion * 3 + axis, 1), :]
                total = total + factor * seen[motion][camera * blocks : (camera + 1) * blocks]
        rows[axis] = total
        copies.append(pltpu.make_async_copy(rows.at[axis], out_ref.at[axis], sems.at[axis]))
        copies[-1].start()
    for copy in copies:
        copy.wait()


def finish(calibration, hot, back, damped, capacity, devices):
    vmem = pl.BlockSpec(memory_space=pltpu.VMEM)
    spread = jnp.broadcast_to(calibration[:, None], (calibration.shape[0], LANES))
    return pl.pallas_call(
        functools.partial(finish_kernel, capacity=capacity, devices=devices),
        in_specs=[vmem, vmem, vmem, vmem],
        out_specs=pl.BlockSpec(memory_space=pl.ANY),
        out_shape=jax.ShapeDtypeStruct(damped.shape, jnp.float32),
        scratch_shapes=[pltpu.VMEM(damped.shape, jnp.float32), pltpu.SemaphoreType.DMA((3,))],
        compiler_params=pltpu.CompilerParams(vmem_limit_bytes=VMEM_LIMIT),
        name="finish",
    )(spread, hot, back, damped)


def exchange(values):
    return lax.all_to_all(values, AXES, split_axis=0, concat_axis=0, tiled=True)


def per_device(images, direction, damping, calibration, camera, owners, local_block, connect):
    devices = lax.axis_size(AXES)
    tiles, listed = owners.shape
    blocks, _, width = direction.shape
    cameras = calibration.shape[0]
    capacity = max(2, min(tiles, 4 * tiles * listed // devices))
    direction = direction.transpose(1, 0, 2)
    damping = damping.transpose(1, 0, 2)
    calibration = calibration.reshape(-1)
    if capacity == tiles:
        wanted = requests(owners, local_block, camera, blocks, devices, cameras * blocks)
        slot = jnp.broadcast_to(jnp.arange(tiles, dtype=jnp.int32)[:, None], owners.shape)
    else:
        everyone = jnp.arange(devices, dtype=jnp.int32)
        code = camera[:, None] * blocks + local_block
        hits = owners[None, :, :] == everyone[:, None, None]
        named = jnp.sum(jnp.where(hits, code[None] + 1, 0), axis=2)
        taken = (named > 0).astype(jnp.int32)
        rank = jnp.cumsum(taken, axis=1) - taken
        slots = jnp.arange(capacity, dtype=jnp.int32)
        chosen = (rank[:, :, None] == slots[None, None, :]) & (taken[:, :, None] > 0)
        wanted = jnp.sum(jnp.where(chosen, named[:, :, None], 0), axis=1)
        wanted = jnp.where(wanted > 0, wanted - 1, cameras * blocks)
        slot = jnp.sum(jnp.where(hits, rank[:, :, None], 0), axis=0)
    places = owners * (2 * capacity) + slot
    asked = exchange(wanted.reshape(devices, 1, capacity)).reshape(devices, capacity)
    table = seen_table(calibration, direction)
    sums = pixel_sums(images)
    outgoing = serve(asked, table)
    shape = (devices, 2 * capacity, width)
    arrived = exchange(outgoing.reshape(shape)).reshape(-1, width)
    hot, damped = hot_table(asked.reshape(-1, LANES), direction, damping, cameras)
    forces = tile_forces(places, arrived, sums, connect.reshape(tiles, 4, SUBS, LANES), capacity)
    back = exchange(forces.reshape(shape)).reshape(-1, width)
    product = finish(calibration, hot, back, damped, capacity, devices)
    return product.transpose(1, 0, 2)


def solution(mesh):
    split = P(AXES)
    return jax.shard_map(
        per_device,
        mesh=mesh,
        in_specs=(split, split, split, P(), split, split, split, split),
        out_specs=split,
        check_vma=False,
    )
```

```python
import functools
import math

import jax
import jax.numpy as jnp
import numpy as np
from jax import lax
from jax.experimental import pallas as pl
from jax.experimental.pallas import tpu as pltpu
from jax.sharding import PartitionSpec as P

EPX = 4
LANES = 128
SUBS = 8
AXES = ("tiles", "nodes")
VMEM_LIMIT = 48 * 1024 * 1024


def pair_weights():
    x = (np.arange(EPX, dtype=np.float64) + 0.5) / EPX
    return np.stack([(1 - x) ** 2, x * (1 - x), x**2])


def column_pool(width):
    cells = width // EPX
    groups = LANES // cells
    weights = pair_weights()
    table = np.zeros((groups, width, 3, groups, cells), np.float32)
    for group in range(groups):
        for pixel in range(width):
            table[group, pixel, :, group, pixel // EPX] = weights[:, pixel % EPX]
    return table.reshape(groups * width, 3 * LANES)


def pixel_kernel(images_ref, pool_ref, out_ref, padded, pooled, *, tiles_step, groups):
    weights = pair_weights()
    height = images_ref.shape[1]
    width = images_ref.shape[2]
    stride = EPX * groups
    lane = lax.broadcasted_iota(jnp.int32, (SUBS, width), 1)
    first = lane == 0
    last = lane == width - 1
    scale = jnp.where(first | last, 1.0, 0.5).astype(jnp.float32)
    for tile in range(tiles_step):
        pixels = images_ref[tile].astype(jnp.float32)
        padded[pl.ds(SUBS, height), :] = pixels
        padded[pl.ds(SUBS - 1, 1), :] = 2.0 * pixels[0:1] - pixels[1:2]
        padded[pl.ds(SUBS + height, 1), :] = 2.0 * pixels[height - 1 :] - pixels[height - 2 : height - 1]
        for group in range(groups):
            sums = [[None] * 3 for _ in range(3)]
            rows = [
                padded[pl.ds(SUBS + group * EPX + step, SUBS, stride=stride), :]
                for step in range(-1, EPX + 1)
            ]
            for step in range(EPX):
                here = rows[step + 1]
                slope_y = 0.5 * (rows[step + 2] - rows[step])
                left = jnp.where(first, here, pltpu.roll(here, 1, 1))
                right = jnp.where(last, here, pltpu.roll(here, width - 1, 1))
                slope_x = scale * (right - left)
                products = (slope_x * slope_x, slope_x * slope_y, slope_y * slope_y)
                for kind in range(3):
                    for pair in range(3):
                        term = float(weights[pair, step]) * products[kind]
                        old = sums[kind][pair]
                        sums[kind][pair] = term if old is None else old + term
            for kind in range(3):
                for pair in range(3):
                    row = (tile * 9 + kind * 3 + pair) * SUBS
                    pooled[pl.ds(row, SUBS), pl.ds(group * width, width)] = sums[kind][pair]
    values = pooled[...]
    high = values.astype(jnp.bfloat16)
    low = (values - high.astype(jnp.float32)).astype(jnp.bfloat16)
    pool = pool_ref[...]
    out_ref[...] = jnp.dot(high, pool, preferred_element_type=jnp.float32) + jnp.dot(
        low, pool, preferred_element_type=jnp.float32
    )


def pixel_sums(images):
    tiles, height, width = images.shape
    groups = LANES * EPX // width
    tiles_step = 4
    rows = tiles_step * 9 * SUBS
    pool = jnp.asarray(column_pool(width), jnp.bfloat16)
    return pl.pallas_call(
        functools.partial(pixel_kernel, tiles_step=tiles_step, groups=groups),
        grid=(tiles // tiles_step,),
        in_specs=[
            pl.BlockSpec((tiles_step, height, width), lambda i: (i, 0, 0)),
            pl.BlockSpec(pool.shape, lambda i: (0, 0)),
        ],
        out_specs=pl.BlockSpec((rows, 3 * LANES), lambda i: (i, 0)),
        out_shape=jax.ShapeDtypeStruct((tiles * 9 * SUBS, 3 * LANES), jnp.float32),
        scratch_shapes=[
            pltpu.VMEM((height + 2 * SUBS, width), jnp.float32),
            pltpu.VMEM((rows, groups * width), jnp.float32),
        ],
        compiler_params=pltpu.CompilerParams(vmem_limit_bytes=VMEM_LIMIT),
        cost_estimate=pl.CostEstimate(
            flops=tiles * 2 * 72 * 512 * 384 * 4, bytes_accessed=4 * images.size, transcendentals=0
        ),
        name="pixel_sums",
    )(images, pool)


def table_kernel(calibration_ref, direction_ref, out_ref):
    blocks = direction_ref.shape[1]
    cameras = calibration_ref.shape[2]
    half = cameras * blocks
    parts = [direction_ref[axis] for axis in range(3)]
    for camera in range(cameras):
        for motion in range(2):
            seen = calibration_ref[0, motion, camera] * parts[0]
            seen = seen + calibration_ref[1, motion, camera] * parts[1]
            seen = seen + calibration_ref[2, motion, camera] * parts[2]
            out_ref[pl.ds(motion * half + camera * blocks, blocks), :] = seen
    out_ref[pl.ds(2 * half, 2 * SUBS), :] = jnp.zeros((2 * SUBS, out_ref.shape[1]), jnp.float32)


def seen_table(calibration, direction):
    _, blocks, width = direction.shape
    cameras = calibration.shape[2]
    return pl.pallas_call(
        table_kernel,
        in_specs=[pl.BlockSpec(memory_space=pltpu.SMEM), pl.BlockSpec(memory_space=pltpu.VMEM)],
        out_specs=pl.BlockSpec(memory_space=pltpu.VMEM),
        out_shape=jax.ShapeDtypeStruct((2 * (cameras * blocks + SUBS), width), jnp.float32),
        compiler_params=pltpu.CompilerParams(vmem_limit_bytes=VMEM_LIMIT),
        cost_estimate=pl.CostEstimate(flops=10**6, bytes_accessed=2 * direction.size, transcendentals=0),
        name="seen_table",
    )(calibration, direction)


def serve_kernel(codes_ref, table_ref, out_ref, rows, sems, *, capacity):
    devices = codes_ref.shape[0] // capacity
    half = table_ref.shape[0] // 2 - SUBS
    pieces = sems.shape[0]
    length = rows.shape[0] // pieces
    copies = []
    for piece in range(pieces):
        for device in range(piece * devices // pieces, (piece + 1) * devices // pieces):
            for slot in range(capacity):
                code = codes_ref[device * capacity + slot]
                for motion in range(2):
                    row = device * (2 * capacity) + motion * capacity + slot
                    rows[pl.ds(row, 1), :] = table_ref[pl.ds(motion * half + code, 1), :]
        place = pl.ds(piece * length, length)
        copies.append(pltpu.make_async_copy(rows.at[place], out_ref.at[place], sems.at[piece]))
        copies[-1].start()
    for copy in copies:
        copy.wait()


def serve(codes, table):
    devices, capacity = codes.shape
    shape = (devices * 2 * capacity, table.shape[1])
    return pl.pallas_call(
        functools.partial(serve_kernel, capacity=capacity),
        in_specs=[pl.BlockSpec(memory_space=pltpu.SMEM), pl.BlockSpec(memory_space=pltpu.VMEM)],
        out_specs=pl.BlockSpec(memory_space=pl.ANY),
        out_shape=jax.ShapeDtypeStruct(shape, jnp.float32),
        scratch_shapes=[pltpu.VMEM(shape, jnp.float32), pltpu.SemaphoreType.DMA((math.gcd(devices, 8),))],
        compiler_params=pltpu.CompilerParams(vmem_limit_bytes=VMEM_LIMIT),
        name="serve",
    )(codes.reshape(-1), table)


def request_kernel(owners_ref, local_ref, camera_ref, out_ref, *, blocks, nothing):
    owners = owners_ref[...].T
    local = local_ref[...].T
    everyone = lax.broadcasted_iota(jnp.int32, out_ref.shape, 0)
    code = camera_ref[...] * blocks
    wanted = jnp.full(out_ref.shape, nothing, jnp.int32)
    for entry in range(owners.shape[0]):
        here = jnp.broadcast_to(owners[entry : entry + 1], out_ref.shape) == everyone
        wanted = jnp.where(here, jnp.broadcast_to(code + local[entry : entry + 1], out_ref.shape), wanted)
    out_ref[...] = wanted


def requests(owners, local_block, camera, blocks, devices, nothing):
    vmem = pl.BlockSpec(memory_space=pltpu.VMEM)
    return pl.pallas_call(
        functools.partial(request_kernel, blocks=blocks, nothing=nothing),
        in_specs=[vmem, vmem, vmem],
        out_specs=vmem,
        out_shape=jax.ShapeDtypeStruct((devices, owners.shape[0]), jnp.int32),
        name="requests",
    )(owners, local_block, camera.reshape(1, -1))


def tile_kernel(place_ref, arrived_ref, sums_ref, connect_ref, out_ref, parts, result, *, capacity, listed, group):
    tiles = connect_ref.shape[0]
    shape = (SUBS, LANES)
    out_ref[...] = jnp.zeros_like(out_ref)

    def one_tile(tile, parts, result):
        links = [connect_ref[tile, corner] for corner in range(4)]
        node_of = [jnp.bitwise_and(link, LANES - 1) for link in links]
        block_of = [jnp.right_shift(link, 7) for link in links]
        motion = [[jnp.zeros(shape, jnp.float32) for _ in range(2)] for _ in range(4)]
        places = [place_ref[tile * listed + entry] for entry in range(listed)]
        for corner in range(4):
            for axis in range(2):
                for entry in range(listed):
                    row = arrived_ref[pl.ds(places[entry] + axis * capacity, 1), :]
                    picked = jnp.take_along_axis(
                        jnp.broadcast_to(row, shape), node_of[corner], axis=1, mode="promise_in_bounds"
                    )
                    motion[corner][axis] = jnp.where(block_of[corner] == entry, picked, motion[corner][axis])

        def element(kind, pair_y, pair_x):
            row = pl.multiple_of(tile * (9 * SUBS), SUBS) + (kind * 3 + pair_y) * SUBS
            return sums_ref[pl.ds(row, SUBS), pl.ds(pair_x * LANES, LANES)]

        for corner in range(4):
            for axis in range(2):
                total = None
                for other in range(4):
                    pair_x = corner % 2 + other % 2
                    pair_y = corner // 2 + other // 2
                    for source in range(2):
                        term = element(axis + source, pair_y, pair_x) * motion[other][source]
                        total = term if total is None else total + term
                high = total.astype(jnp.bfloat16).astype(jnp.float32)
                row = (corner * 4 + axis * 2) * SUBS
                parts[pl.ds(row, SUBS), :] = high
                parts[pl.ds(row + SUBS, SUBS), :] = total - high

        node_ids = lax.broadcasted_iota(jnp.int32, (LANES, LANES), 0).astype(jnp.float32).astype(jnp.bfloat16)
        one, zero = jnp.ones((), jnp.bfloat16), jnp.zeros((), jnp.bfloat16)
        block_ids = lax.broadcasted_iota(jnp.int32, (listed, LANES), 0)
        wide = []
        picks = []
        for corner in range(4):
            hots = []
            spreads = []
            for chunk in range(SUBS):
                link = connect_ref[tile, corner, pl.ds(chunk, 1), :]
                nodes = jnp.bitwise_and(link, LANES - 1).astype(jnp.float32)
                nodes = jnp.broadcast_to(nodes, (2 * SUBS, LANES)).astype(jnp.bfloat16)
                hots.append(
                    jnp.concatenate(
                        [
                            jnp.where(nodes == node_ids[row : row + 2 * SUBS], one, zero)
                            for row in range(0, LANES, 2 * SUBS)
                        ],
                        axis=0,
                    )
                )
                here = jnp.broadcast_to(jnp.right_shift(link, 7), (listed, LANES)) == block_ids
                chosen = []
                for part in range(4):
                    row = parts[pl.ds((corner * 4 + part) * SUBS + chunk, 1), :]
                    chosen.append(jnp.where(here, jnp.broadcast_to(row, (listed, LANES)), 0.0).astype(jnp.bfloat16))
                spreads.append(jnp.concatenate(chosen, axis=0))
            wide.append(jnp.concatenate(spreads, axis=1))
            picks.append(jnp.concatenate(hots, axis=1))
        both = [None, None]
        for pair in range(2):
            right = jnp.concatenate(wide[2 * pair : 2 * pair + 2], axis=0)
            for side in range(2):
                term = lax.dot_general(
                    picks[2 * pair + side], right, (((1,), (1,)), ((), ())), preferred_element_type=jnp.float32
                )
                both[side] = term if both[side] is None else both[side] + term
        total = both[0].T[: 4 * listed] + both[1].T[4 * listed :]
        for axis in range(2):
            base = 2 * axis * listed
            result[pl.ds(axis * listed, listed), :] = (
                total[base : base + listed] + total[base + listed : base + 2 * listed]
            )
        for entry in range(listed):
            for axis in range(2):
                out_ref[pl.ds(places[entry] + axis * capacity, 1), :] = result[pl.ds(axis * listed + entry, 1), :]

    def one_group(step, carry):
        for member in range(group):
            one_tile(step * group + member, parts.at[member], result.at[member])
        return carry

    lax.fori_loop(0, tiles // group, one_group, 0)


def tile_forces(places, arrived, sums, connect, capacity):
    tiles, listed = places.shape
    group = math.gcd(tiles, 16)
    vmem = pl.BlockSpec(memory_space=pltpu.VMEM)
    return pl.pallas_call(
        functools.partial(tile_kernel, capacity=capacity, listed=listed, group=group),
        in_specs=[pl.BlockSpec(memory_space=pltpu.SMEM), vmem, vmem, vmem],
        out_specs=vmem,
        out_shape=jax.ShapeDtypeStruct(arrived.shape, jnp.float32),
        scratch_shapes=[
            pltpu.VMEM((group, 16 * SUBS, LANES), jnp.float32),
            pltpu.VMEM((group, 2 * listed, LANES), jnp.float32),
        ],
        compiler_params=pltpu.CompilerParams(vmem_limit_bytes=VMEM_LIMIT),
        name="tile_forces",
    )(places.reshape(-1), arrived, sums, connect)


def hot_kernel(codes_ref, direction_ref, damping_ref, hot_ref, damped_ref):
    for part in range(codes_ref.shape[0]):
        ids = lax.broadcasted_iota(jnp.int32, (hot_ref.shape[0], LANES), 0)
        here = jnp.broadcast_to(codes_ref[pl.ds(part, 1), :], ids.shape) == ids
        hot_ref[:, pl.ds(part * LANES, LANES)] = jnp.where(here, 1.0, 0.0).astype(jnp.bfloat16)
    damped_ref[...] = damping_ref[...] * direction_ref[...]


def hot_table(codes, direction, damping, cameras):
    vmem = pl.BlockSpec(memory_space=pltpu.VMEM)
    shape = (cameras * direction.shape[1], codes.size)
    return pl.pallas_call(
        hot_kernel,
        in_specs=[vmem, vmem, vmem],
        out_specs=(vmem, vmem),
        out_shape=(
            jax.ShapeDtypeStruct(shape, jnp.bfloat16),
            jax.ShapeDtypeStruct(direction.shape, jnp.float32),
        ),
        compiler_params=pltpu.CompilerParams(vmem_limit_bytes=VMEM_LIMIT),
        cost_estimate=pl.CostEstimate(flops=10**6, bytes_accessed=10**6, transcendentals=0),
        name="hot_table",
    )(codes, direction, damping)


def finish_kernel(calibration_ref, hot_ref, back_ref, damped_ref, out_ref, rows, sems, *, capacity, devices):
    blocks = damped_ref.shape[1]
    cameras = calibration_ref.shape[0] // 6
    slots = devices * capacity
    back = back_ref[...].reshape(devices, 2, capacity, LANES)
    halves = []
    for motion in range(2):
        values = back[:, motion].reshape(slots, LANES)
        high = values.astype(jnp.bfloat16)
        halves += [high, (values - high.astype(jnp.float32)).astype(jnp.bfloat16)]
    right = jnp.concatenate(halves, axis=1)
    summed = jnp.dot(hot_ref[...], right, preferred_element_type=jnp.float32)
    seen = []
    for motion in range(2):
        base = 2 * motion * LANES
        seen.append(summed[:, base : base + LANES] + summed[:, base + LANES : base + 2 * LANES])
    copies = []
    for axis in range(3):
        total = damped_ref[axis]
        for camera in range(cameras):
            for motion in range(2):
                factor = calibration_ref[pl.ds(camera * 6 + motion * 3 + axis, 1), :]
                total = total + factor * seen[motion][camera * blocks : (camera + 1) * blocks]
        rows[axis] = total
        copies.append(pltpu.make_async_copy(rows.at[axis], out_ref.at[axis], sems.at[axis]))
        copies[-1].start()
    for copy in copies:
        copy.wait()


def finish(calibration, hot, back, damped, capacity, devices):
    vmem = pl.BlockSpec(memory_space=pltpu.VMEM)
    spread = jnp.broadcast_to(calibration[:, None], (calibration.shape[0], LANES))
    return pl.pallas_call(
        functools.partial(finish_kernel, capacity=capacity, devices=devices),
        in_specs=[vmem, vmem, vmem, vmem],
        out_specs=pl.BlockSpec(memory_space=pl.ANY),
        out_shape=jax.ShapeDtypeStruct(damped.shape, jnp.float32),
        scratch_shapes=[pltpu.VMEM(damped.shape, jnp.float32), pltpu.SemaphoreType.DMA((3,))],
        compiler_params=pltpu.CompilerParams(vmem_limit_bytes=VMEM_LIMIT),
        name="finish",
    )(spread, hot, back, damped)


def exchange(values):
    return lax.all_to_all(values, AXES, split_axis=0, concat_axis=0, tiled=True)


def per_device(images, direction, damping, calibration, camera, owners, local_block, connect):
    devices = lax.axis_size(AXES)
    tiles, listed = owners.shape
    blocks, _, width = direction.shape
    cameras = calibration.shape[0]
    capacity = max(2, min(tiles, 4 * tiles * listed // devices))
    direction = direction.transpose(1, 0, 2)
    damping = damping.transpose(1, 0, 2)
    if capacity == tiles:
        wanted = requests(owners, local_block, camera, blocks, devices, cameras * blocks)
        slot = jnp.broadcast_to(jnp.arange(tiles, dtype=jnp.int32)[:, None], owners.shape)
    else:
        everyone = jnp.arange(devices, dtype=jnp.int32)
        code = camera[:, None] * blocks + local_block
        hits = owners[None, :, :] == everyone[:, None, None]
        named = jnp.sum(jnp.where(hits, code[None] + 1, 0), axis=2)
        taken = (named > 0).astype(jnp.int32)
        rank = jnp.cumsum(taken, axis=1) - taken
        slots = jnp.arange(capacity, dtype=jnp.int32)
        chosen = (rank[:, :, None] == slots[None, None, :]) & (taken[:, :, None] > 0)
        wanted = jnp.sum(jnp.where(chosen, named[:, :, None], 0), axis=1)
        wanted = jnp.where(wanted > 0, wanted - 1, cameras * blocks)
        slot = jnp.sum(jnp.where(hits, rank[:, :, None], 0), axis=0)
    places = owners * (2 * capacity) + slot
    asked = exchange(wanted.reshape(devices, 1, capacity)).reshape(devices, capacity)
    table = seen_table(calibration.transpose(2, 1, 0), direction)
    sums = pixel_sums(images)
    outgoing = serve(asked, table)
    shape = (devices, 2 * capacity, width)
    arrived = exchange(outgoing.reshape(shape)).reshape(-1, width)
    hot, damped = hot_table(asked.reshape(-1, LANES), direction, damping, cameras)
    forces = tile_forces(places, arrived, sums, connect.reshape(tiles, 4, SUBS, LANES), capacity)
    back = exchange(forces.reshape(shape)).reshape(-1, width)
    product = finish(calibration.reshape(-1), hot, back, damped, capacity, devices)
    return product.transpose(1, 0, 2)


def solution(mesh):
    split = P(AXES)
    return jax.shard_map(
        per_device,
        mesh=mesh,
        in_specs=(split, split, split, P(), split, split, split, split),
        out_specs=split,
        check_vma=False,
    )
```

```python
import functools
import math

import jax
import jax.numpy as jnp
import numpy as np
from jax import lax
from jax.experimental import pallas as pl
from jax.experimental.pallas import tpu as pltpu
from jax.sharding import PartitionSpec as P

EPX = 4
LANES = 128
SUBS = 8
AXES = ("tiles", "nodes")
VMEM_LIMIT = 48 * 1024 * 1024


def pair_weights():
    x = (np.arange(EPX, dtype=np.float64) + 0.5) / EPX
    return np.stack([(1 - x) ** 2, x * (1 - x), x**2])


def column_pool(width):
    cells = width // EPX
    groups = LANES // cells
    weights = pair_weights()
    table = np.zeros((groups, width, 3, groups, cells), np.float32)
    for group in range(groups):
        for pixel in range(width):
            table[group, pixel, :, group, pixel // EPX] = weights[:, pixel % EPX]
    return table.reshape(groups * width, 3 * LANES)


def pixel_kernel(images_ref, pool_ref, out_ref, padded, pooled, *, tiles_step, groups):
    weights = pair_weights()
    height = images_ref.shape[1]
    width = images_ref.shape[2]
    stride = EPX * groups
    lane = lax.broadcasted_iota(jnp.int32, (SUBS, width), 1)
    first = lane == 0
    last = lane == width - 1
    scale = jnp.where(first | last, 1.0, 0.5).astype(jnp.float32)
    for tile in range(tiles_step):
        pixels = images_ref[tile].astype(jnp.float32)
        padded[pl.ds(SUBS, height), :] = pixels
        padded[pl.ds(SUBS - 1, 1), :] = 2.0 * pixels[0:1] - pixels[1:2]
        padded[pl.ds(SUBS + height, 1), :] = 2.0 * pixels[height - 1 :] - pixels[height - 2 : height - 1]
        for group in range(groups):
            sums = [[None] * 3 for _ in range(3)]
            rows = [
                padded[pl.ds(SUBS + group * EPX + step, SUBS, stride=stride), :]
                for step in range(-1, EPX + 1)
            ]
            for step in range(EPX):
                here = rows[step + 1]
                slope_y = 0.5 * (rows[step + 2] - rows[step])
                left = jnp.where(first, here, pltpu.roll(here, 1, 1))
                right = jnp.where(last, here, pltpu.roll(here, width - 1, 1))
                slope_x = scale * (right - left)
                products = (slope_x * slope_x, slope_x * slope_y, slope_y * slope_y)
                for kind in range(3):
                    for pair in range(3):
                        term = float(weights[pair, step]) * products[kind]
                        old = sums[kind][pair]
                        sums[kind][pair] = term if old is None else old + term
            for kind in range(3):
                for pair in range(3):
                    row = (tile * 9 + kind * 3 + pair) * SUBS
                    pooled[pl.ds(row, SUBS), pl.ds(group * width, width)] = sums[kind][pair]
    values = pooled[...]
    high = values.astype(jnp.bfloat16)
    low = (values - high.astype(jnp.float32)).astype(jnp.bfloat16)
    pool = pool_ref[...]
    out_ref[...] = jnp.dot(high, pool, preferred_element_type=jnp.float32) + jnp.dot(
        low, pool, preferred_element_type=jnp.float32
    )


def pixel_sums(images):
    tiles, height, width = images.shape
    groups = LANES * EPX // width
    tiles_step = 4
    rows = tiles_step * 9 * SUBS
    pool = jnp.asarray(column_pool(width), jnp.bfloat16)
    return pl.pallas_call(
        functools.partial(pixel_kernel, tiles_step=tiles_step, groups=groups),
        grid=(tiles // tiles_step,),
        in_specs=[
            pl.BlockSpec((tiles_step, height, width), lambda i: (i, 0, 0)),
            pl.BlockSpec(pool.shape, lambda i: (0, 0)),
        ],
        out_specs=pl.BlockSpec((rows, 3 * LANES), lambda i: (i, 0)),
        out_shape=jax.ShapeDtypeStruct((tiles * 9 * SUBS, 3 * LANES), jnp.float32),
        scratch_shapes=[
            pltpu.VMEM((height + 2 * SUBS, width), jnp.float32),
            pltpu.VMEM((rows, groups * width), jnp.float32),
        ],
        compiler_params=pltpu.CompilerParams(vmem_limit_bytes=VMEM_LIMIT),
        cost_estimate=pl.CostEstimate(
            flops=tiles * 2 * 72 * 512 * 384 * 4, bytes_accessed=4 * images.size, transcendentals=0
        ),
        name="pixel_sums",
    )(images, pool)


def table_kernel(calibration_ref, direction_ref, out_ref):
    blocks = direction_ref.shape[1]
    cameras = calibration_ref.shape[2]
    half = cameras * blocks
    parts = [direction_ref[axis] for axis in range(3)]
    for camera in range(cameras):
        for motion in range(2):
            seen = calibration_ref[0, motion, camera] * parts[0]
            seen = seen + calibration_ref[1, motion, camera] * parts[1]
            seen = seen + calibration_ref[2, motion, camera] * parts[2]
            out_ref[pl.ds(motion * half + camera * blocks, blocks), :] = seen
    out_ref[pl.ds(2 * half, 2 * SUBS), :] = jnp.zeros((2 * SUBS, out_ref.shape[1]), jnp.float32)


def seen_table(calibration, direction):
    _, blocks, width = direction.shape
    cameras = calibration.shape[2]
    return pl.pallas_call(
        table_kernel,
        in_specs=[pl.BlockSpec(memory_space=pltpu.SMEM), pl.BlockSpec(memory_space=pltpu.VMEM)],
        out_specs=pl.BlockSpec(memory_space=pltpu.VMEM),
        out_shape=jax.ShapeDtypeStruct((2 * (cameras * blocks + SUBS), width), jnp.float32),
        compiler_params=pltpu.CompilerParams(vmem_limit_bytes=VMEM_LIMIT),
        cost_estimate=pl.CostEstimate(flops=10**6, bytes_accessed=2 * direction.size, transcendentals=0),
        name="seen_table",
    )(calibration, direction)


def serve_kernel(codes_ref, table_ref, out_ref, rows, sems, *, capacity):
    devices = codes_ref.shape[0] // capacity
    half = table_ref.shape[0] // 2 - SUBS
    pieces = sems.shape[0]
    length = rows.shape[0] // pieces
    copies = []
    for piece in range(pieces):
        for device in range(piece * devices // pieces, (piece + 1) * devices // pieces):
            for slot in range(capacity):
                code = codes_ref[device * capacity + slot]
                for motion in range(2):
                    row = device * (2 * capacity) + motion * capacity + slot
                    rows[pl.ds(row, 1), :] = table_ref[pl.ds(motion * half + code, 1), :]
        place = pl.ds(piece * length, length)
        copies.append(pltpu.make_async_copy(rows.at[place], out_ref.at[place], sems.at[piece]))
        copies[-1].start()
    for copy in copies:
        copy.wait()


def serve(codes, table):
    devices, capacity = codes.shape
    shape = (devices * 2 * capacity, table.shape[1])
    return pl.pallas_call(
        functools.partial(serve_kernel, capacity=capacity),
        in_specs=[pl.BlockSpec(memory_space=pltpu.SMEM), pl.BlockSpec(memory_space=pltpu.VMEM)],
        out_specs=pl.BlockSpec(memory_space=pl.ANY),
        out_shape=jax.ShapeDtypeStruct(shape, jnp.float32),
        scratch_shapes=[pltpu.VMEM(shape, jnp.float32), pltpu.SemaphoreType.DMA((math.gcd(devices, 8),))],
        compiler_params=pltpu.CompilerParams(vmem_limit_bytes=VMEM_LIMIT),
        name="serve",
    )(codes.reshape(-1), table)


def request_kernel(owners_ref, local_ref, camera_ref, out_ref, *, blocks, nothing):
    owners = owners_ref[...].T
    local = local_ref[...].T
    everyone = lax.broadcasted_iota(jnp.int32, out_ref.shape, 0)
    code = camera_ref[...] * blocks
    wanted = jnp.full(out_ref.shape, nothing, jnp.int32)
    for entry in range(owners.shape[0]):
        here = jnp.broadcast_to(owners[entry : entry + 1], out_ref.shape) == everyone
        wanted = jnp.where(here, jnp.broadcast_to(code + local[entry : entry + 1], out_ref.shape), wanted)
    out_ref[...] = wanted


def requests(owners, local_block, camera, blocks, devices, nothing):
    vmem = pl.BlockSpec(memory_space=pltpu.VMEM)
    return pl.pallas_call(
        functools.partial(request_kernel, blocks=blocks, nothing=nothing),
        in_specs=[vmem, vmem, vmem],
        out_specs=vmem,
        out_shape=jax.ShapeDtypeStruct((devices, owners.shape[0]), jnp.int32),
        name="requests",
    )(owners, local_block, camera.reshape(1, -1))


def tile_kernel(place_ref, arrived_ref, sums_ref, connect_ref, out_ref, parts, result, *, capacity, listed, group):
    tiles = connect_ref.shape[0]
    shape = (SUBS, LANES)
    out_ref[...] = jnp.zeros_like(out_ref)

    def one_tile(tile, parts, result):
        links = [connect_ref[tile, corner] for corner in range(4)]
        node_of = [jnp.bitwise_and(link, LANES - 1) for link in links]
        block_of = [jnp.right_shift(link, 7) for link in links]
        motion = [[jnp.zeros(shape, jnp.float32) for _ in range(2)] for _ in range(4)]
        places = [place_ref[tile * listed + entry] for entry in range(listed)]
        for corner in range(4):
            for axis in range(2):
                for entry in range(listed):
                    row = arrived_ref[pl.ds(places[entry] + axis * capacity, 1), :]
                    picked = jnp.take_along_axis(
                        jnp.broadcast_to(row, shape), node_of[corner], axis=1, mode="promise_in_bounds"
                    )
                    motion[corner][axis] = jnp.where(block_of[corner] == entry, picked, motion[corner][axis])

        def element(kind, pair_y, pair_x):
            row = pl.multiple_of(tile * (9 * SUBS), SUBS) + (kind * 3 + pair_y) * SUBS
            return sums_ref[pl.ds(row, SUBS), pl.ds(pair_x * LANES, LANES)]

        for corner in range(4):
            for axis in range(2):
                total = None
                for other in range(4):
                    pair_x = corner % 2 + other % 2
                    pair_y = corner // 2 + other // 2
                    for source in range(2):
                        term = element(axis + source, pair_y, pair_x) * motion[other][source]
                        total = term if total is None else total + term
                high = total.astype(jnp.bfloat16).astype(jnp.float32)
                row = (corner * 4 + axis * 2) * SUBS
                parts[pl.ds(row, SUBS), :] = high
                parts[pl.ds(row + SUBS, SUBS), :] = total - high

        node_ids = lax.broadcasted_iota(jnp.int32, (LANES, LANES), 0).astype(jnp.float32).astype(jnp.bfloat16)
        one, zero = jnp.ones((), jnp.bfloat16), jnp.zeros((), jnp.bfloat16)
        block_ids = lax.broadcasted_iota(jnp.int32, (listed, LANES), 0).astype(jnp.float32).astype(jnp.bfloat16)
        wide = []
        picks = []
        for corner in range(4):
            hots = []
            spreads = []
            for chunk in range(SUBS):
                link = connect_ref[tile, corner, pl.ds(chunk, 1), :]
                nodes = jnp.bitwise_and(link, LANES - 1).astype(jnp.float32)
                nodes = jnp.broadcast_to(nodes, (2 * SUBS, LANES)).astype(jnp.bfloat16)
                hots.append(
                    jnp.concatenate(
                        [
                            jnp.where(nodes == node_ids[row : row + 2 * SUBS], one, zero)
                            for row in range(0, LANES, 2 * SUBS)
                        ],
                        axis=0,
                    )
                )
                block = jnp.right_shift(link, 7).astype(jnp.float32)
                here = jnp.broadcast_to(block, (listed, LANES)).astype(jnp.bfloat16) == block_ids
                chosen = []
                for part in range(4):
                    row = parts[pl.ds((corner * 4 + part) * SUBS + chunk, 1), :]
                    chosen.append(jnp.where(here, jnp.broadcast_to(row, (listed, LANES)).astype(jnp.bfloat16), zero))
                spreads.append(jnp.concatenate(chosen, axis=0))
            wide.append(jnp.concatenate(spreads, axis=1))
            picks.append(jnp.concatenate(hots, axis=1))
        both = [None, None]
        for pair in range(2):
            right = jnp.concatenate(wide[2 * pair : 2 * pair + 2], axis=0)
            for side in range(2):
                term = lax.dot_general(
                    picks[2 * pair + side], right, (((1,), (1,)), ((), ())), preferred_element_type=jnp.float32
                )
                both[side] = term if both[side] is None else both[side] + term
        total = both[0].T[: 4 * listed] + both[1].T[4 * listed :]
        for axis in range(2):
            base = 2 * axis * listed
            result[pl.ds(axis * listed, listed), :] = (
                total[base : base + listed] + total[base + listed : base + 2 * listed]
            )
        for entry in range(listed):
            for axis in range(2):
                out_ref[pl.ds(places[entry] + axis * capacity, 1), :] = result[pl.ds(axis * listed + entry, 1), :]

    def one_group(step, carry):
        for member in range(group):
            one_tile(step * group + member, parts.at[member], result.at[member])
        return carry

    lax.fori_loop(0, tiles // group, one_group, 0)


def tile_forces(places, arrived, sums, connect, capacity):
    tiles, listed = places.shape
    group = math.gcd(tiles, 16)
    vmem = pl.BlockSpec(memory_space=pltpu.VMEM)
    return pl.pallas_call(
        functools.partial(tile_kernel, capacity=capacity, listed=listed, group=group),
        in_specs=[pl.BlockSpec(memory_space=pltpu.SMEM), vmem, vmem, vmem],
        out_specs=vmem,
        out_shape=jax.ShapeDtypeStruct(arrived.shape, jnp.float32),
        scratch_shapes=[
            pltpu.VMEM((group, 16 * SUBS, LANES), jnp.float32),
            pltpu.VMEM((group, 2 * listed, LANES), jnp.float32),
        ],
        compiler_params=pltpu.CompilerParams(vmem_limit_bytes=VMEM_LIMIT),
        name="tile_forces",
    )(places.reshape(-1), arrived, sums, connect)


def hot_kernel(codes_ref, direction_ref, damping_ref, hot_ref, damped_ref):
    for part in range(codes_ref.shape[0]):
        ids = lax.broadcasted_iota(jnp.int32, (hot_ref.shape[0], LANES), 0)
        here = jnp.broadcast_to(codes_ref[pl.ds(part, 1), :], ids.shape) == ids
        hot_ref[:, pl.ds(part * LANES, LANES)] = jnp.where(here, 1.0, 0.0).astype(jnp.bfloat16)
    damped_ref[...] = damping_ref[...] * direction_ref[...]


def hot_table(codes, direction, damping, cameras):
    vmem = pl.BlockSpec(memory_space=pltpu.VMEM)
    shape = (cameras * direction.shape[1], codes.size)
    return pl.pallas_call(
        hot_kernel,
        in_specs=[vmem, vmem, vmem],
        out_specs=(vmem, vmem),
        out_shape=(
            jax.ShapeDtypeStruct(shape, jnp.bfloat16),
            jax.ShapeDtypeStruct(direction.shape, jnp.float32),
        ),
        compiler_params=pltpu.CompilerParams(vmem_limit_bytes=VMEM_LIMIT),
        cost_estimate=pl.CostEstimate(flops=10**6, bytes_accessed=10**6, transcendentals=0),
        name="hot_table",
    )(codes, direction, damping)


def finish_kernel(calibration_ref, hot_ref, back_ref, damped_ref, out_ref, rows, sems, *, capacity, devices):
    blocks = damped_ref.shape[1]
    cameras = calibration_ref.shape[0] // 6
    slots = devices * capacity
    back = back_ref[...].reshape(devices, 2, capacity, LANES)
    halves = []
    for motion in range(2):
        values = back[:, motion].reshape(slots, LANES)
        high = values.astype(jnp.bfloat16)
        halves += [high, (values - high.astype(jnp.float32)).astype(jnp.bfloat16)]
    right = jnp.concatenate(halves, axis=1)
    summed = jnp.dot(hot_ref[...], right, preferred_element_type=jnp.float32)
    seen = []
    for motion in range(2):
        base = 2 * motion * LANES
        seen.append(summed[:, base : base + LANES] + summed[:, base + LANES : base + 2 * LANES])
    copies = []
    for axis in range(3):
        total = damped_ref[axis]
        for camera in range(cameras):
            for motion in range(2):
                factor = calibration_ref[pl.ds(camera * 6 + motion * 3 + axis, 1), :]
                total = total + factor * seen[motion][camera * blocks : (camera + 1) * blocks]
        rows[axis] = total
        copies.append(pltpu.make_async_copy(rows.at[axis], out_ref.at[axis], sems.at[axis]))
        copies[-1].start()
    for copy in copies:
        copy.wait()


def finish(calibration, hot, back, damped, capacity, devices):
    vmem = pl.BlockSpec(memory_space=pltpu.VMEM)
    spread = jnp.broadcast_to(calibration[:, None], (calibration.shape[0], LANES))
    return pl.pallas_call(
        functools.partial(finish_kernel, capacity=capacity, devices=devices),
        in_specs=[vmem, vmem, vmem, vmem],
        out_specs=pl.BlockSpec(memory_space=pl.ANY),
        out_shape=jax.ShapeDtypeStruct(damped.shape, jnp.float32),
        scratch_shapes=[pltpu.VMEM(damped.shape, jnp.float32), pltpu.SemaphoreType.DMA((3,))],
        compiler_params=pltpu.CompilerParams(vmem_limit_bytes=VMEM_LIMIT),
        name="finish",
    )(spread, hot, back, damped)


def exchange(values):
    return lax.all_to_all(values, AXES, split_axis=0, concat_axis=0, tiled=True)


def per_device(images, direction, damping, calibration, camera, owners, local_block, connect):
    devices = lax.axis_size(AXES)
    tiles, listed = owners.shape
    blocks, _, width = direction.shape
    cameras = calibration.shape[0]
    capacity = max(2, min(tiles, 4 * tiles * listed // devices))
    direction = direction.transpose(1, 0, 2)
    damping = damping.transpose(1, 0, 2)
    if capacity == tiles:
        wanted = requests(owners, local_block, camera, blocks, devices, cameras * blocks)
        slot = jnp.broadcast_to(jnp.arange(tiles, dtype=jnp.int32)[:, None], owners.shape)
    else:
        everyone = jnp.arange(devices, dtype=jnp.int32)
        code = camera[:, None] * blocks + local_block
        hits = owners[None, :, :] == everyone[:, None, None]
        named = jnp.sum(jnp.where(hits, code[None] + 1, 0), axis=2)
        taken = (named > 0).astype(jnp.int32)
        rank = jnp.cumsum(taken, axis=1) - taken
        slots = jnp.arange(capacity, dtype=jnp.int32)
        chosen = (rank[:, :, None] == slots[None, None, :]) & (taken[:, :, None] > 0)
        wanted = jnp.sum(jnp.where(chosen, named[:, :, None], 0), axis=1)
        wanted = jnp.where(wanted > 0, wanted - 1, cameras * blocks)
        slot = jnp.sum(jnp.where(hits, rank[:, :, None], 0), axis=0)
    places = owners * (2 * capacity) + slot
    asked = exchange(wanted.reshape(devices, 1, capacity)).reshape(devices, capacity)
    table = seen_table(calibration.transpose(2, 1, 0), direction)
    sums = pixel_sums(images)
    outgoing = serve(asked, table)
    shape = (devices, 2 * capacity, width)
    arrived = exchange(outgoing.reshape(shape)).reshape(-1, width)
    hot, damped = hot_table(asked.reshape(-1, LANES), direction, damping, cameras)
    forces = tile_forces(places, arrived, sums, connect.reshape(tiles, 4, SUBS, LANES), capacity)
    back = exchange(forces.reshape(shape)).reshape(-1, width)
    product = finish(calibration.reshape(-1), hot, back, damped, capacity, devices)
    return product.transpose(1, 0, 2)


def solution(mesh):
    split = P(AXES)
    return jax.shard_map(
        per_device,
        mesh=mesh,
        in_specs=(split, split, split, P(), split, split, split, split),
        out_specs=split,
        check_vma=False,
    )
```

```python
import functools
import math

import jax
import jax.numpy as jnp
import numpy as np
from jax import lax
from jax.experimental import pallas as pl
from jax.experimental.pallas import tpu as pltpu
from jax.sharding import PartitionSpec as P

EPX = 4
LANES = 128
SUBS = 8
AXES = ("tiles", "nodes")
VMEM_LIMIT = 48 * 1024 * 1024


def pair_weights():
    x = (np.arange(EPX, dtype=np.float64) + 0.5) / EPX
    return np.stack([(1 - x) ** 2, x * (1 - x), x**2])


def column_pool(width):
    cells = width // EPX
    groups = LANES // cells
    weights = pair_weights()
    table = np.zeros((groups, width, 3, groups, cells), np.float32)
    for group in range(groups):
        for pixel in range(width):
            table[group, pixel, :, group, pixel // EPX] = weights[:, pixel % EPX]
    return table.reshape(groups * width, 3 * LANES)


def pixel_kernel(images_ref, pool_ref, out_ref, padded, pooled, *, tiles_step, groups):
    weights = pair_weights()
    height = images_ref.shape[1]
    width = images_ref.shape[2]
    stride = EPX * groups
    lane = lax.broadcasted_iota(jnp.int32, (SUBS, width), 1)
    first = lane == 0
    last = lane == width - 1
    scale = jnp.where(first | last, 1.0, 0.5).astype(jnp.float32)
    for tile in range(tiles_step):
        pixels = images_ref[tile].astype(jnp.float32)
        padded[pl.ds(SUBS, height), :] = pixels
        padded[pl.ds(SUBS - 1, 1), :] = 2.0 * pixels[0:1] - pixels[1:2]
        padded[pl.ds(SUBS + height, 1), :] = 2.0 * pixels[height - 1 :] - pixels[height - 2 : height - 1]
        for group in range(groups):
            sums = [[None] * 3 for _ in range(3)]
            rows = [
                padded[pl.ds(SUBS + group * EPX + step, SUBS, stride=stride), :]
                for step in range(-1, EPX + 1)
            ]
            for step in range(EPX):
                here = rows[step + 1]
                slope_y = 0.5 * (rows[step + 2] - rows[step])
                left = jnp.where(first, here, pltpu.roll(here, 1, 1))
                right = jnp.where(last, here, pltpu.roll(here, width - 1, 1))
                slope_x = scale * (right - left)
                products = (slope_x * slope_x, slope_x * slope_y, slope_y * slope_y)
                for kind in range(3):
                    for pair in range(3):
                        term = float(weights[pair, step]) * products[kind]
                        old = sums[kind][pair]
                        sums[kind][pair] = term if old is None else old + term
            for kind in range(3):
                for pair in range(3):
                    row = (tile * 9 + kind * 3 + pair) * SUBS
                    pooled[pl.ds(row, SUBS), pl.ds(group * width, width)] = sums[kind][pair]
    values = pooled[...]
    high = values.astype(jnp.bfloat16)
    low = (values - high.astype(jnp.float32)).astype(jnp.bfloat16)
    pool = pool_ref[...]
    out_ref[...] = jnp.dot(high, pool, preferred_element_type=jnp.float32) + jnp.dot(
        low, pool, preferred_element_type=jnp.float32
    )


def pixel_sums(images):
    tiles, height, width = images.shape
    groups = LANES * EPX // width
    tiles_step = 4
    rows = tiles_step * 9 * SUBS
    pool = jnp.asarray(column_pool(width), jnp.bfloat16)
    return pl.pallas_call(
        functools.partial(pixel_kernel, tiles_step=tiles_step, groups=groups),
        grid=(tiles // tiles_step,),
        in_specs=[
            pl.BlockSpec((tiles_step, height, width), lambda i: (i, 0, 0)),
            pl.BlockSpec(pool.shape, lambda i: (0, 0)),
        ],
        out_specs=pl.BlockSpec((rows, 3 * LANES), lambda i: (i, 0)),
        out_shape=jax.ShapeDtypeStruct((tiles * 9 * SUBS, 3 * LANES), jnp.float32),
        scratch_shapes=[
            pltpu.VMEM((height + 2 * SUBS, width), jnp.float32),
            pltpu.VMEM((rows, groups * width), jnp.float32),
        ],
        compiler_params=pltpu.CompilerParams(vmem_limit_bytes=VMEM_LIMIT),
        cost_estimate=pl.CostEstimate(
            flops=tiles * 2 * 72 * 512 * 384 * 4, bytes_accessed=4 * images.size, transcendentals=0
        ),
        name="pixel_sums",
    )(images, pool)


def table_kernel(calibration_ref, direction_ref, out_ref):
    blocks = direction_ref.shape[1]
    cameras = calibration_ref.shape[2]
    half = cameras * blocks
    parts = [direction_ref[axis] for axis in range(3)]
    for camera in range(cameras):
        for motion in range(2):
            seen = calibration_ref[0, motion, camera] * parts[0]
            seen = seen + calibration_ref[1, motion, camera] * parts[1]
            seen = seen + calibration_ref[2, motion, camera] * parts[2]
            out_ref[pl.ds(motion * half + camera * blocks, blocks), :] = seen
    out_ref[pl.ds(2 * half, 2 * SUBS), :] = jnp.zeros((2 * SUBS, out_ref.shape[1]), jnp.float32)


def seen_table(calibration, direction):
    _, blocks, width = direction.shape
    cameras = calibration.shape[2]
    return pl.pallas_call(
        table_kernel,
        in_specs=[pl.BlockSpec(memory_space=pltpu.SMEM), pl.BlockSpec(memory_space=pltpu.VMEM)],
        out_specs=pl.BlockSpec(memory_space=pltpu.VMEM),
        out_shape=jax.ShapeDtypeStruct((2 * (cameras * blocks + SUBS), width), jnp.float32),
        compiler_params=pltpu.CompilerParams(vmem_limit_bytes=VMEM_LIMIT),
        cost_estimate=pl.CostEstimate(flops=10**6, bytes_accessed=2 * direction.size, transcendentals=0),
        name="seen_table",
    )(calibration, direction)


def serve_kernel(codes_ref, table_ref, out_ref, rows, sems, *, capacity):
    devices = codes_ref.shape[0] // capacity
    half = table_ref.shape[0] // 2 - SUBS
    pieces = sems.shape[0]
    length = rows.shape[0] // pieces
    copies = []
    for piece in range(pieces):
        for device in range(piece * devices // pieces, (piece + 1) * devices // pieces):
            for slot in range(capacity):
                code = codes_ref[device * capacity + slot]
                for motion in range(2):
                    row = device * (2 * capacity) + motion * capacity + slot
                    rows[pl.ds(row, 1), :] = table_ref[pl.ds(motion * half + code, 1), :]
        place = pl.ds(piece * length, length)
        copies.append(pltpu.make_async_copy(rows.at[place], out_ref.at[place], sems.at[piece]))
        copies[-1].start()
    for copy in copies:
        copy.wait()


def serve(codes, table):
    devices, capacity = codes.shape
    shape = (devices * 2 * capacity, table.shape[1])
    return pl.pallas_call(
        functools.partial(serve_kernel, capacity=capacity),
        in_specs=[pl.BlockSpec(memory_space=pltpu.SMEM), pl.BlockSpec(memory_space=pltpu.VMEM)],
        out_specs=pl.BlockSpec(memory_space=pl.ANY),
        out_shape=jax.ShapeDtypeStruct(shape, jnp.float32),
        scratch_shapes=[pltpu.VMEM(shape, jnp.float32), pltpu.SemaphoreType.DMA((math.gcd(devices, 4),))],
        compiler_params=pltpu.CompilerParams(vmem_limit_bytes=VMEM_LIMIT),
        name="serve",
    )(codes.reshape(-1), table)


def request_kernel(owners_ref, local_ref, camera_ref, out_ref, *, blocks, nothing):
    owners = owners_ref[...].T
    local = local_ref[...].T
    everyone = lax.broadcasted_iota(jnp.int32, out_ref.shape, 0)
    code = camera_ref[...] * blocks
    wanted = jnp.full(out_ref.shape, nothing, jnp.int32)
    for entry in range(owners.shape[0]):
        here = jnp.broadcast_to(owners[entry : entry + 1], out_ref.shape) == everyone
        wanted = jnp.where(here, jnp.broadcast_to(code + local[entry : entry + 1], out_ref.shape), wanted)
    out_ref[...] = wanted


def requests(owners, local_block, camera, blocks, devices, nothing):
    vmem = pl.BlockSpec(memory_space=pltpu.VMEM)
    return pl.pallas_call(
        functools.partial(request_kernel, blocks=blocks, nothing=nothing),
        in_specs=[vmem, vmem, vmem],
        out_specs=vmem,
        out_shape=jax.ShapeDtypeStruct((devices, owners.shape[0]), jnp.int32),
        name="requests",
    )(owners, local_block, camera.reshape(1, -1))


def tile_kernel(place_ref, arrived_ref, sums_ref, connect_ref, out_ref, parts, result, *, capacity, listed, group):
    tiles = connect_ref.shape[0]
    shape = (SUBS, LANES)
    out_ref[...] = jnp.zeros_like(out_ref)

    def one_tile(tile, parts, result):
        links = [connect_ref[tile, corner] for corner in range(4)]
        node_of = [jnp.bitwise_and(link, LANES - 1) for link in links]
        block_of = [jnp.right_shift(link, 7) for link in links]
        motion = [[jnp.zeros(shape, jnp.float32) for _ in range(2)] for _ in range(4)]
        places = [place_ref[tile * listed + entry] for entry in range(listed)]
        for corner in range(4):
            for axis in range(2):
                for entry in range(listed):
                    row = arrived_ref[pl.ds(places[entry] + axis * capacity, 1), :]
                    picked = jnp.take_along_axis(
                        jnp.broadcast_to(row, shape), node_of[corner], axis=1, mode="promise_in_bounds"
                    )
                    motion[corner][axis] = jnp.where(block_of[corner] == entry, picked, motion[corner][axis])

        def element(kind, pair_y, pair_x):
            row = pl.multiple_of(tile * (9 * SUBS), SUBS) + (kind * 3 + pair_y) * SUBS
            return sums_ref[pl.ds(row, SUBS), pl.ds(pair_x * LANES, LANES)]

        for corner in range(4):
            for axis in range(2):
                total = None
                for other in range(4):
                    pair_x = corner % 2 + other % 2
                    pair_y = corner // 2 + other // 2
                    for source in range(2):
                        term = element(axis + source, pair_y, pair_x) * motion[other][source]
                        total = term if total is None else total + term
                high = total.astype(jnp.bfloat16).astype(jnp.float32)
                row = (corner * 4 + axis * 2) * SUBS
                parts[pl.ds(row, SUBS), :] = high
                parts[pl.ds(row + SUBS, SUBS), :] = total - high

        node_ids = lax.broadcasted_iota(jnp.int32, (LANES, LANES), 0).astype(jnp.float32).astype(jnp.bfloat16)
        one, zero = jnp.ones((), jnp.bfloat16), jnp.zeros((), jnp.bfloat16)
        block_ids = lax.broadcasted_iota(jnp.int32, (listed, LANES), 0)
        wide = []
        picks = []
        for corner in range(4):
            hots = []
            spreads = []
            for chunk in range(SUBS):
                link = connect_ref[tile, corner, pl.ds(chunk, 1), :]
                nodes = jnp.bitwise_and(link, LANES - 1).astype(jnp.float32)
                nodes = jnp.broadcast_to(nodes, (2 * SUBS, LANES)).astype(jnp.bfloat16)
                hots.append(
                    jnp.concatenate(
                        [
                            jnp.where(nodes == node_ids[row : row + 2 * SUBS], one, zero)
                            for row in range(0, LANES, 2 * SUBS)
                        ],
                        axis=0,
                    )
                )
                here = jnp.broadcast_to(jnp.right_shift(link, 7), (listed, LANES)) == block_ids
                chosen = []
                for part in range(4):
                    row = parts[pl.ds((corner * 4 + part) * SUBS + chunk, 1), :]
                    chosen.append(jnp.where(here, jnp.broadcast_to(row, (listed, LANES)), 0.0).astype(jnp.bfloat16))
                spreads.append(jnp.concatenate(chosen, axis=0))
            wide.append(jnp.concatenate(spreads, axis=1))
            picks.append(jnp.concatenate(hots, axis=1))
        both = [None, None]
        for pair in range(2):
            right = jnp.concatenate(wide[2 * pair : 2 * pair + 2], axis=0)
            for side in range(2):
                term = lax.dot_general(
                    picks[2 * pair + side], right, (((1,), (1,)), ((), ())), preferred_element_type=jnp.float32
                )
                both[side] = term if both[side] is None else both[side] + term
        total = both[0].T[: 4 * listed] + both[1].T[4 * listed :]
        for axis in range(2):
            base = 2 * axis * listed
            result[pl.ds(axis * listed, listed), :] = (
                total[base : base + listed] + total[base + listed : base + 2 * listed]
            )
        for entry in range(listed):
            for axis in range(2):
                out_ref[pl.ds(places[entry] + axis * capacity, 1), :] = result[pl.ds(axis * listed + entry, 1), :]

    def one_group(step, carry):
        for member in range(group):
            one_tile(step * group + member, parts.at[member], result.at[member])
        return carry

    lax.fori_loop(0, tiles // group, one_group, 0)


def tile_forces(places, arrived, sums, connect, capacity):
    tiles, listed = places.shape
    group = math.gcd(tiles, 16)
    vmem = pl.BlockSpec(memory_space=pltpu.VMEM)
    return pl.pallas_call(
        functools.partial(tile_kernel, capacity=capacity, listed=listed, group=group),
        in_specs=[pl.BlockSpec(memory_space=pltpu.SMEM), vmem, vmem, vmem],
        out_specs=vmem,
        out_shape=jax.ShapeDtypeStruct(arrived.shape, jnp.float32),
        scratch_shapes=[
            pltpu.VMEM((group, 16 * SUBS, LANES), jnp.float32),
            pltpu.VMEM((group, 2 * listed, LANES), jnp.float32),
        ],
        compiler_params=pltpu.CompilerParams(vmem_limit_bytes=VMEM_LIMIT),
        name="tile_forces",
    )(places.reshape(-1), arrived, sums, connect)


def hot_kernel(codes_ref, direction_ref, damping_ref, hot_ref, damped_ref):
    for part in range(codes_ref.shape[0]):
        ids = lax.broadcasted_iota(jnp.int32, (hot_ref.shape[0], LANES), 0)
        here = jnp.broadcast_to(codes_ref[pl.ds(part, 1), :], ids.shape) == ids
        hot_ref[:, pl.ds(part * LANES, LANES)] = jnp.where(here, 1.0, 0.0).astype(jnp.bfloat16)
    damped_ref[...] = damping_ref[...] * direction_ref[...]


def hot_table(codes, direction, damping, cameras):
    vmem = pl.BlockSpec(memory_space=pltpu.VMEM)
    shape = (cameras * direction.shape[1], codes.size)
    return pl.pallas_call(
        hot_kernel,
        in_specs=[vmem, vmem, vmem],
        out_specs=(vmem, vmem),
        out_shape=(
            jax.ShapeDtypeStruct(shape, jnp.bfloat16),
            jax.ShapeDtypeStruct(direction.shape, jnp.float32),
        ),
        compiler_params=pltpu.CompilerParams(vmem_limit_bytes=VMEM_LIMIT),
        cost_estimate=pl.CostEstimate(flops=10**6, bytes_accessed=10**6, transcendentals=0),
        name="hot_table",
    )(codes, direction, damping)


def finish_kernel(calibration_ref, hot_ref, back_ref, damped_ref, out_ref, rows, sems, *, capacity, devices):
    blocks = damped_ref.shape[1]
    cameras = calibration_ref.shape[0] // 6
    slots = devices * capacity
    back = back_ref[...].reshape(devices, 2, capacity, LANES)
    halves = []
    for motion in range(2):
        values = back[:, motion].reshape(slots, LANES)
        high = values.astype(jnp.bfloat16)
        halves += [high, (values - high.astype(jnp.float32)).astype(jnp.bfloat16)]
    right = jnp.concatenate(halves, axis=1)
    summed = jnp.dot(hot_ref[...], right, preferred_element_type=jnp.float32)
    seen = []
    for motion in range(2):
        base = 2 * motion * LANES
        seen.append(summed[:, base : base + LANES] + summed[:, base + LANES : base + 2 * LANES])
    copies = []
    for axis in range(3):
        total = damped_ref[axis]
        for camera in range(cameras):
            for motion in range(2):
                factor = calibration_ref[pl.ds(camera * 6 + motion * 3 + axis, 1), :]
                total = total + factor * seen[motion][camera * blocks : (camera + 1) * blocks]
        rows[axis] = total
        copies.append(pltpu.make_async_copy(rows.at[axis], out_ref.at[axis], sems.at[axis]))
        copies[-1].start()
    for copy in copies:
        copy.wait()


def finish(calibration, hot, back, damped, capacity, devices):
    vmem = pl.BlockSpec(memory_space=pltpu.VMEM)
    spread = jnp.broadcast_to(calibration[:, None], (calibration.shape[0], LANES))
    return pl.pallas_call(
        functools.partial(finish_kernel, capacity=capacity, devices=devices),
        in_specs=[vmem, vmem, vmem, vmem],
        out_specs=pl.BlockSpec(memory_space=pl.ANY),
        out_shape=jax.ShapeDtypeStruct(damped.shape, jnp.float32),
        scratch_shapes=[pltpu.VMEM(damped.shape, jnp.float32), pltpu.SemaphoreType.DMA((3,))],
        compiler_params=pltpu.CompilerParams(vmem_limit_bytes=VMEM_LIMIT),
        name="finish",
    )(spread, hot, back, damped)


def exchange(values):
    return lax.all_to_all(values, AXES, split_axis=0, concat_axis=0, tiled=True)


def per_device(images, direction, damping, calibration, camera, owners, local_block, connect):
    devices = lax.axis_size(AXES)
    tiles, listed = owners.shape
    blocks, _, width = direction.shape
    cameras = calibration.shape[0]
    capacity = max(2, min(tiles, 4 * tiles * listed // devices))
    direction = direction.transpose(1, 0, 2)
    damping = damping.transpose(1, 0, 2)
    if capacity == tiles:
        wanted = requests(owners, local_block, camera, blocks, devices, cameras * blocks)
        slot = jnp.broadcast_to(jnp.arange(tiles, dtype=jnp.int32)[:, None], owners.shape)
    else:
        everyone = jnp.arange(devices, dtype=jnp.int32)
        code = camera[:, None] * blocks + local_block
        hits = owners[None, :, :] == everyone[:, None, None]
        named = jnp.sum(jnp.where(hits, code[None] + 1, 0), axis=2)
        taken = (named > 0).astype(jnp.int32)
        rank = jnp.cumsum(taken, axis=1) - taken
        slots = jnp.arange(capacity, dtype=jnp.int32)
        chosen = (rank[:, :, None] == slots[None, None, :]) & (taken[:, :, None] > 0)
        wanted = jnp.sum(jnp.where(chosen, named[:, :, None], 0), axis=1)
        wanted = jnp.where(wanted > 0, wanted - 1, cameras * blocks)
        slot = jnp.sum(jnp.where(hits, rank[:, :, None], 0), axis=0)
    places = owners * (2 * capacity) + slot
    asked = exchange(wanted.reshape(devices, 1, capacity)).reshape(devices, capacity)
    table = seen_table(calibration.transpose(2, 1, 0), direction)
    sums = pixel_sums(images)
    outgoing = serve(asked, table)
    shape = (devices, 2 * capacity, width)
    arrived = exchange(outgoing.reshape(shape)).reshape(-1, width)
    hot, damped = hot_table(asked.reshape(-1, LANES), direction, damping, cameras)
    forces = tile_forces(places, arrived, sums, connect.reshape(tiles, 4, SUBS, LANES), capacity)
    back = exchange(forces.reshape(shape)).reshape(-1, width)
    product = finish(calibration.reshape(-1), hot, back, damped, capacity, devices)
    return product.transpose(1, 0, 2)


def solution(mesh):
    split = P(AXES)
    return jax.shard_map(
        per_device,
        mesh=mesh,
        in_specs=(split, split, split, P(), split, split, split, split),
        out_specs=split,
        check_vma=False,
    )
```
